512 devices in a mesh: batch: 32 (over z, core), tensor: 16 (over y, x).
Axes of the slice: x: 4, y: 4, z: 16, core: 2. Of those that a mesh axis runs over, the one named last changes fastest.
Arguments:
- tokens: bfloat16 [640, 8192], P('tensor', 'batch'), may hold values from -32 to 32
- norm_gain: float32 [8192], P('batch'), may hold values from 0.1 to 1.9
- in_x_weight: bfloat16 [8192, 8192], P('batch', 'tensor'), may hold values from -0.0625 to 0.0625
- in_z_weight: bfloat16 [8192, 8192], P('batch', 'tensor'), may hold values from -0.0625 to 0.0625
- conv_state: bfloat16 [3, 640, 8192], P(None, 'batch', 'tensor'), may hold values from -6 to 6
- conv_weight: float32 [4, 8192], P(None, 'tensor'), may hold values from -3 to 3
- conv_bias: float32 [8192], P('tensor'), may hold values from -1 to 1
- proj_weight: bfloat16 [8192, 544], P('tensor'), may hold values from -0.0625 to 0.0625
- delta_weight: bfloat16 [512, 8192], P(None, 'tensor'), may hold values from -0.25 to 0.25
- delta_bias: float32 [8192], P('tensor'), may hold values from -4 to 0
- decay_log: float32 [16, 8192], P(None, 'tensor'), may hold values from 0 to 2.77
- ssm_state: float32 [640, 16, 8192], P('batch', None, 'tensor'), may hold values from -6 to 6
- skip_gain: float32 [8192], P('tensor'), may hold values from 0.5 to 1.5
- out_weight: bfloat16 [8192, 8192], P('tensor', 'batch'), may hold values from -0.0625 to 0.0625
- post_gain: float32 [8192], P('batch'), may hold values from 0.1 to 1.9
- gate_weight: bfloat16 [8192, 12288], P('batch', 'tensor'), may hold values from -0.0625 to 0.0625
- up_weight: bfloat16 [8192, 12288], P('batch', 'tensor'), may hold values from -0.0625 to 0.0625
- down_weight: bfloat16 [12288, 8192], P('tensor', 'batch'), may hold values from -0.0546875 to 0.0546875
Outputs:
- mixed: bfloat16 [640, 8192], P('tensor', 'batch')
- new_conv_state: bfloat16 [3, 640, 8192], P(None, 'batch', 'tensor')
- new_state: float32 [640, 16, 8192], P('batch', None, 'tensor')
The draws below stay inside these ranges and needn't reach their ends.
All inputs are finite; a program needn't handle non-finite values.
Results may differ from the reference program's by a relative error of at most 0.03.
Values may be sent and summed in bfloat16 or wider, within the bound.
No kernel may reach another device: no remote copies, remote signals or barrier semaphores. Data moves between devices by JAX's collectives and lax.ppermute only.
A program may use at most 64 MiB of HBM per device.

```python
import jax
import jax.numpy as jnp
from jax import lax

WIDTH = 8192
INNER = 8192
FFN = 12288
RANK = 512
STATE = 16
KERNEL = 4
ROWS = 640
N_BATCH = 32
N_TENSOR = 16


def draw_tokens(key, part):
    key = jax.random.fold_in(key, 11)
    first_key, second_key, third_key = jax.random.split(key, 3)
    ramp = jnp.arange(WIDTH, dtype=jnp.float32) / WIDTH
    column_scale = 10.0 ** (0.5 * ramp + 0.5 * jax.random.uniform(second_key, (WIDTH,), jnp.float32) - 0.5)
    row_scale = 10.0 ** (jax.random.uniform(third_key, (ROWS, 1), jnp.float32) - 0.5)
    base = jnp.clip(jax.random.normal(first_key, (ROWS, WIDTH), jnp.float32), -2.5, 2.5)
    return (base * row_scale * column_scale[None, :]).astype(jnp.bfloat16)


def level_of(stream_key, extent, cuts, least, high):
    def one(dim, blocks):
        steps = jax.random.uniform(jax.random.fold_in(jax.random.fold_in(stream_key, 6), dim), (blocks,), jnp.float32, least / len(cuts), high / len(cuts))
        return jnp.repeat(jnp.exp(steps), extent[dim] // blocks).reshape((-1,) + (1,) * (len(extent) - dim - 1))

    loudness = one(*cuts[0])
    for cut in cuts[1:]:
        loudness = loudness * one(*cut)
    return loudness


def scatter_about(rng, dims, scale, limit, shards=(), kind=jnp.bfloat16):
    entries = scale * jax.random.normal(rng, dims, jnp.float32)
    if shards:
        entries = entries * level_of(rng, dims, shards, -0.22, 0.18)
    return jnp.clip(entries, -limit, limit).astype(kind)


def setup_inputs(seed: int = 0) -> dict:
    arg_keys = jax.random.split(jax.random.key(seed), 19)
    tokens = draw_tokens(jax.random.fold_in(arg_keys[18], 71), 0)
    norm_gain = jnp.clip(1.0 + 0.18 * jax.random.normal(arg_keys[1], (WIDTH,), jnp.float32), 0.1, 1.9)
    in_x_weight = scatter_about(arg_keys[2], (WIDTH, INNER), WIDTH ** -0.5, 0.0625, ((0, 32), (1, 16)))
    in_z_weight = scatter_about(arg_keys[3], (WIDTH, INNER), WIDTH ** -0.5, 0.0625, ((0, 32), (1, 16)))
    conv_state = scatter_about(arg_keys[4], (KERNEL - 1, ROWS, INNER), 1.0, 6.0, ((1, 32), (2, 16)))
    conv_weight = scatter_about(arg_keys[5], (KERNEL, INNER), KERNEL ** -0.5, 3.0, ((1, 16),), jnp.float32)
    conv_bias = jnp.clip(jax.random.uniform(arg_keys[6], (INNER,), jnp.float32, -1.0, 1.0) * level_of(arg_keys[6], (INNER,), ((0, 16),), -0.4, 0.0), -1.0, 1.0)
    proj_weight = scatter_about(arg_keys[7], (INNER, RANK + 2 * STATE), INNER ** -0.5, 0.0625, ((0, 16),))
    delta_weight = scatter_about(arg_keys[8], (RANK, INNER), RANK ** -0.5, 0.25, ((1, 16),))
    delta_bias = jnp.clip(-4.0 + 4.0 * jax.random.uniform(arg_keys[9], (INNER,), jnp.float32) ** level_of(arg_keys[9], (INNER,), ((0, 16),), -0.2, 0.2), -4.0, 0.0)
    decay_log = jnp.clip(2.77 * jax.random.uniform(arg_keys[10], (STATE, INNER), jnp.float32) ** level_of(arg_keys[10], (STATE, INNER), ((1, 16),), -0.2, 0.2), 0.0, 2.77)
    ssm_state = scatter_about(arg_keys[11], (ROWS, STATE, INNER), 1.0, 6.0, ((0, 32), (2, 16)), jnp.float32)
    skip_gain = jnp.clip(0.5 + 1.0 * jax.random.uniform(arg_keys[12], (INNER,), jnp.float32) ** level_of(arg_keys[12], (INNER,), ((0, 16),), -0.2, 0.2), 0.5, 1.5)
    out_weight = scatter_about(arg_keys[13], (INNER, WIDTH), INNER ** -0.5, 0.0625, ((0, 16), (1, 32)))
    post_gain = jnp.clip(1.0 + 0.18 * jax.random.normal(arg_keys[14], (WIDTH,), jnp.float32), 0.1, 1.9)
    gate_weight = scatter_about(arg_keys[15], (WIDTH, FFN), WIDTH ** -0.5, 0.0625, ((0, 32), (1, 16)))
    up_weight = scatter_about(arg_keys[16], (WIDTH, FFN), WIDTH ** -0.5, 0.0625, ((0, 32), (1, 16)))
    down_weight = scatter_about(arg_keys[17], (FFN, WIDTH), FFN ** -0.5, 0.0546875, ((0, 16), (1, 32)))
    return dict(tokens=tokens, norm_gain=norm_gain, in_x_weight=in_x_weight, in_z_weight=in_z_weight, conv_state=conv_state, conv_weight=conv_weight, conv_bias=conv_bias, proj_weight=proj_weight, delta_weight=delta_weight, delta_bias=delta_bias, decay_log=decay_log, ssm_state=ssm_state, skip_gain=skip_gain, out_weight=out_weight, post_gain=post_gain, gate_weight=gate_weight, up_weight=up_weight, down_weight=down_weight)


epsilon = 1e-06

def block_sum(left, right, parts):
    size = left.shape[1] // parts

    def step(total, index):
        start = (index * size).astype(jnp.int32)
        left_block = lax.dynamic_slice_in_dim(left, start, size, 1)
        right_block = lax.dynamic_slice_in_dim(right, start, size, 0)
        term = jnp.dot(left_block, right_block, preferred_element_type=jnp.float32).astype(jnp.bfloat16)
        term = lax.optimization_barrier(term)
        return (total + term.astype(jnp.float32), None)
    zero = jnp.zeros((left.shape[0], right.shape[1]), jnp.float32)
    total, _ = lax.scan(step, zero, jnp.arange(parts, dtype=jnp.int32))
    return total

def rms_scale(values):
    return lax.rsqrt(lax.optimization_barrier(jnp.mean(values * values, axis=1, keepdims=True)) + epsilon)

def reference(tokens, norm_gain, in_x_weight, in_z_weight, conv_state, conv_weight, conv_bias, proj_weight, delta_weight, delta_bias, decay_log, ssm_state, skip_gain, out_weight, post_gain, gate_weight, up_weight, down_weight):
    wide = tokens.astype(jnp.float32)
    normed = (wide * rms_scale(wide) * norm_gain[None, :]).astype(jnp.bfloat16)
    inner_x = block_sum(normed, in_x_weight, N_BATCH).astype(jnp.bfloat16)
    gate_z = block_sum(normed, in_z_weight, N_BATCH).astype(jnp.bfloat16)
    window = jnp.concatenate([conv_state, inner_x[None]], axis=0)
    conv_pre = lax.optimization_barrier(jnp.sum(window.astype(jnp.float32) * conv_weight[:, None, :], axis=0)) + conv_bias[None, :]
    signal = jax.nn.silu(conv_pre).astype(jnp.bfloat16)
    projected = jnp.dot(signal, proj_weight, preferred_element_type=jnp.float32)
    delta_low = projected[:, :RANK]
    input_map = projected[:, RANK:RANK + STATE]
    output_map = projected[:, RANK + STATE:]
    delta_norm = (delta_low * rms_scale(delta_low)).astype(jnp.bfloat16)
    delta = jax.nn.softplus(jnp.dot(delta_norm, delta_weight, preferred_element_type=jnp.float32) + delta_bias[None, :])
    signal_wide = signal.astype(jnp.float32)
    decay = jnp.exp(delta[:, None, :] * (-jnp.exp(decay_log))[None, :, :])
    new_state = decay * ssm_state + (delta * signal_wide)[:, None, :] * input_map[:, :, None]
    readout = lax.optimization_barrier(jnp.sum(new_state * output_map[:, :, None], axis=1)) + skip_gain[None, :] * signal_wide
    gated = (readout * jax.nn.silu(gate_z.astype(jnp.float32))).astype(jnp.bfloat16)
    residual = (wide + block_sum(gated, out_weight, N_TENSOR)).astype(jnp.bfloat16)
    residual_wide = residual.astype(jnp.float32)
    post = (residual_wide * rms_scale(residual_wide) * post_gain[None, :]).astype(jnp.bfloat16)
    gate = block_sum(post, gate_weight, N_BATCH)
    upper = block_sum(post, up_weight, N_BATCH)
    active = (jax.nn.silu(gate) * upper).astype(jnp.bfloat16)
    mixed = (residual_wide + block_sum(active, down_weight, N_TENSOR)).astype(jnp.bfloat16)
    return (mixed, window[1:], new_state)
```

```python
import jax
import jax.numpy as jnp
import numpy as np
from jax import lax
from jax.sharding import Mesh, PartitionSpec as P

WIDTH = 8192
RANK = 512
STATE = 16

epsilon = 1e-06

F32 = jnp.float32
BF16 = jnp.bfloat16
ROW_MAJOR = ("y", "x")
ROW_SWAPPED = ("x", "y")
RING = ("zh", "zl")


def spread(block, axes, count):
    return lax.all_to_all(jnp.broadcast_to(block[None], (count,) + block.shape), axes, 0, 0)


def swap_cores(block):
    return lax.ppermute(block, "c", [(0, 1), (1, 0)])


def dot(left, right):
    return jnp.dot(left, right, preferred_element_type=F32)


def half_columns(weight, which):
    half = weight.shape[1] // 2
    return lax.dynamic_slice_in_dim(weight, which * half, half, 1)


def reduce_rows(rows, gain, left_weight, right_weight, core):
    blocks, size, depth = rows.shape
    wide = rows.astype(F32)
    scaled = (wide * gain[None, None, :]).astype(BF16).reshape(blocks * size, depth)
    squares = jnp.sum(wide * wide, axis=2).reshape(4, 4, size)

    def partial(which):
        weight = jnp.concatenate(
            [half_columns(left_weight, which), half_columns(right_weight, which)], axis=1
        )
        return dot(scaled, weight).astype(BF16).reshape(4, 4 * size, -1)

    other = partial(1 - core)
    columns = other.shape[2]
    tail = jnp.pad(squares.astype(BF16), ((0, 0), (0, 4), (0, columns - size)))
    received = swap_cores(jnp.concatenate([other, tail], axis=1))
    own = jnp.concatenate([partial(core), tail], axis=1)
    total = (own.astype(F32) + received.astype(F32)).astype(BF16)
    near = jnp.sum(lax.all_to_all(total, "zl", 0, 0).astype(F32), axis=0).astype(BF16)
    near_rows = near[: 4 * size].reshape(4, size, columns)
    near_tail = jnp.pad(near[4 * size : 4 * size + 4][:, None, :], ((0, 0), (0, 7), (0, 0)))
    far = lax.all_to_all(jnp.concatenate([near_rows, near_tail], axis=1), "zh", 0, 0)
    far = jnp.sum(far.astype(F32), axis=0)
    return far[:size], far[size, :size]


def on_device(
    tokens,
    norm_gain,
    in_x_weight,
    in_z_weight,
    conv_state,
    conv_weight,
    conv_bias,
    proj_weight,
    delta_weight,
    delta_bias,
    decay_log,
    ssm_state,
    skip_gain,
    out_weight,
    post_gain,
    gate_weight,
    up_weight,
    down_weight,
):
    core = lax.axis_index("c")
    inner_dev = in_x_weight.shape[1]
    half = inner_dev // 2
    own_rows = conv_state.shape[1]
    token_rows, token_cols = tokens.shape

    gathered = spread(tokens, ROW_SWAPPED, 16)
    sums, first = reduce_rows(gathered, norm_gain, in_x_weight, in_z_weight, core)
    scale = lax.rsqrt(first / WIDTH + epsilon)[:, None]
    mixed_in = (sums * scale).astype(BF16)
    mine = lax.dynamic_slice_in_dim(mixed_in, core * own_rows, own_rows, 0)
    theirs = swap_cores(lax.dynamic_slice_in_dim(mixed_in, (1 - core) * own_rows, own_rows, 0))
    low = jnp.where(core == 0, mine, theirs)
    high = jnp.where(core == 0, theirs, mine)
    inner_x = jnp.concatenate([low[:, :half], high[:, :half]], axis=1)
    gate_z = jnp.concatenate([low[:, half:], high[:, half:]], axis=1)
    window = jnp.concatenate([conv_state, inner_x[None]], axis=0)
    conv_pre = jnp.sum(window.astype(F32) * conv_weight[:, None, :], axis=0) + conv_bias[None, :]
    signal = jax.nn.silu(conv_pre).astype(BF16)
    projected = jnp.sum(
        spread(dot(signal, proj_weight).astype(BF16), ROW_MAJOR, 16).astype(F32), axis=0
    )
    delta_low = projected[:, :RANK]
    input_map = projected[:, RANK : RANK + STATE]
    output_map = projected[:, RANK + STATE :]
    delta_scale = lax.rsqrt(jnp.mean(delta_low * delta_low, axis=1, keepdims=True) + epsilon)
    delta_norm = (delta_low * delta_scale).astype(BF16)
    delta = jax.nn.softplus(dot(delta_norm, delta_weight) + delta_bias[None, :])
    signal_wide = signal.astype(F32)
    decay = jnp.exp(delta[:, None, :] * (-jnp.exp(decay_log))[None, :, :])
    new_state = decay * ssm_state + (delta * signal_wide)[:, None, :] * input_map[:, :, None]
    readout = jnp.sum(new_state * output_map[:, :, None], axis=1) + skip_gain[None, :] * signal_wide
    gated = (readout * jax.nn.silu(gate_z.astype(F32))).astype(BF16)

    same = spread(gated, RING, 16)
    other = swap_cores(same)
    rows = jnp.concatenate(
        [jnp.where(core == 0, same, other), jnp.where(core == 0, other, same)], axis=1
    )
    out_terms = dot(rows.reshape(16 * token_rows, inner_dev), out_weight).astype(BF16)
    out_own = jnp.sum(
        lax.all_to_all(out_terms.reshape(16, token_rows, token_cols), ROW_MAJOR, 0, 0).astype(F32),
        axis=0,
    )
    residual = (tokens.astype(F32) + out_own).astype(BF16)

    gathered = spread(residual, ROW_SWAPPED, 16)
    sums, second = reduce_rows(gathered, post_gain, gate_weight, up_weight, core)
    scale = lax.rsqrt(second / WIDTH + epsilon)[:, None]
    hidden = gate_weight.shape[1] // 2
    both = sums * scale
    active = (jax.nn.silu(both[:, :hidden]) * both[:, hidden:]).astype(BF16)
    same = spread(active, RING, 16)
    other = swap_cores(same)
    same = same.reshape(16 * token_rows, hidden)
    other = other.reshape(16 * token_rows, hidden)
    down_terms = dot(same, lax.dynamic_slice_in_dim(down_weight, core * hidden, hidden, 0)) + dot(
        other, lax.dynamic_slice_in_dim(down_weight, (1 - core) * hidden, hidden, 0)
    )
    down_own = jnp.sum(
        lax.all_to_all(
            down_terms.astype(BF16).reshape(16, token_rows, token_cols), ROW_MAJOR, 0, 0
        ).astype(F32),
        axis=0,
    )
    mixed = (residual.astype(F32) + down_own).astype(BF16)
    return (mixed, window[1:], new_state)


def solution(mesh):
    fine = Mesh(np.asarray(mesh.devices).reshape(4, 4, 2, 4, 4), ("zh", "zl", "c", "y", "x"))
    batch, tensor = ("zh", "zl", "c"), ("y", "x")
    return jax.shard_map(
        on_device,
        mesh=fine,
        in_specs=(
            P(tensor, batch),
            P(batch),
            P(batch, tensor),
            P(batch, tensor),
            P(None, batch, tensor),
            P(None, tensor),
            P(tensor),
            P(tensor, None),
            P(None, tensor),
            P(tensor),
            P(None, tensor),
            P(batch, None, tensor),
            P(tensor),
            P(tensor, batch),
            P(batch),
            P(batch, tensor),
            P(batch, tensor),
            P(tensor, batch),
        ),
        out_specs=(P(tensor, batch), P(None, batch, tensor), P(batch, None, tensor)),
        check_vma=False,
    )
```

```python
import jax
import jax.numpy as jnp
import numpy as np
from jax import lax
from jax.sharding import Mesh, PartitionSpec as P

WIDTH = 8192
RANK = 512
STATE = 16

epsilon = 1e-06

F32 = jnp.float32
BF16 = jnp.bfloat16
TENSOR = ("y", "xm", "xp")
TENSOR_PAIRS = ("xp", "y", "xm")
RING = ("zh", "zm", "zp")
PAIRS = ("zh", "zm")


def spread(block, axes, count):
    return lax.all_to_all(jnp.broadcast_to(block[None], (count,) + block.shape), axes, 0, 0)


def swap(block, axis):
    return lax.ppermute(block, axis, [(0, 1), (1, 0)])


def dot(left, right):
    return jnp.dot(left, right, preferred_element_type=F32)


def add(left, right):
    return (left.astype(F32) + right.astype(F32)).astype(BF16)


def half_columns(weight, which):
    half = weight.shape[1] // 2
    return lax.dynamic_slice_in_dim(weight, which * half, half, 1)


def half_rows(block, which):
    half = block.shape[0] // 2
    return lax.dynamic_slice_in_dim(block, which * half, half, 0)


def reduce_rows(block, size, gain, left_weight, right_weight, axes):
    core, pair = lax.axis_index("c"), lax.axis_index("zp")
    groups, padded, depth = block.shape
    wide = spread(block.reshape(groups * padded, depth), TENSOR_PAIRS, 16).astype(F32)
    scaled = (wide * gain[None, None, :]).astype(BF16).reshape(16 * groups * padded, depth)
    squares = jnp.sum(wide * wide, axis=2).reshape(16 * groups, 1, padded)
    half = left_weight.shape[1] // 2
    columns = half + half
    marks = jnp.pad(squares.astype(BF16), ((0, 0), (0, 0), (0, columns - padded)))
    spare = lax.broadcasted_iota(jnp.int32, (1, padded, columns), 1) == size

    def partial(which):
        weight = jnp.concatenate(
            [half_columns(left_weight, which), half_columns(right_weight, which)], axis=1
        )
        return jnp.where(
            spare, marks, dot(scaled, weight).astype(BF16).reshape(16 * groups, padded, columns)
        )

    received = swap(partial(1 - core), "c")
    own = partial(core)
    sent = add(half_rows(own, 1 - pair), half_rows(received, 1 - pair))
    kept = add(half_rows(own, pair), half_rows(received, pair))
    total = add(kept, swap(sent, "zp"))
    far = lax.all_to_all(total, axes, 0, 0).astype(F32)
    return jnp.sum(far.reshape(8, groups, padded, columns), axis=0)


def on_device(
    tokens,
    norm_gain,
    in_x_weight,
    in_z_weight,
    conv_state,
    conv_weight,
    conv_bias,
    proj_weight,
    delta_weight,
    delta_bias,
    decay_log,
    ssm_state,
    skip_gain,
    out_weight,
    post_gain,
    gate_weight,
    up_weight,
    down_weight,
):
    core, pair = lax.axis_index("c"), lax.axis_index("zp")
    inner_dev = in_x_weight.shape[1]
    half = inner_dev // 2
    own_rows = conv_state.shape[1]
    token_rows, token_cols = tokens.shape

    block = jnp.pad(tokens.reshape(2, own_rows, token_cols), ((0, 0), (0, 4), (0, 0)))
    sums = reduce_rows(
        block, own_rows, norm_gain, in_x_weight, in_z_weight, ("zh", "zm", "c")
    )
    scale = lax.rsqrt(sums[0, own_rows, :own_rows] / WIDTH + epsilon)[:, None]
    mixed_in = (sums[:, :own_rows] * scale[None]).astype(BF16)
    inner_x = jnp.concatenate([mixed_in[0, :, :half], mixed_in[1, :, :half]], axis=1)
    gate_z = jnp.concatenate([mixed_in[0, :, half:], mixed_in[1, :, half:]], axis=1)
    window = jnp.concatenate([conv_state, inner_x[None]], axis=0)
    conv_pre = jnp.sum(window.astype(F32) * conv_weight[:, None, :], axis=0) + conv_bias[None, :]
    signal = jax.nn.silu(conv_pre).astype(BF16)
    projected = jnp.sum(
        spread(dot(signal, proj_weight).astype(BF16), TENSOR, 16).astype(F32), axis=0
    )
    delta_low = projected[:, :RANK]
    input_map = projected[:, RANK : RANK + STATE]
    output_map = projected[:, RANK + STATE :]
    delta_scale = lax.rsqrt(jnp.mean(delta_low * delta_low, axis=1, keepdims=True) + epsilon)
    delta_norm = (delta_low * delta_scale).astype(BF16)
    delta = jax.nn.softplus(dot(delta_norm, delta_weight) + delta_bias[None, :])
    signal_wide = signal.astype(F32)
    decay = jnp.exp(delta[:, None, :] * (-jnp.exp(decay_log))[None, :, :])
    new_state = decay * ssm_state + (delta * signal_wide)[:, None, :] * input_map[:, :, None]
    readout = jnp.sum(new_state * output_map[:, :, None], axis=1) + skip_gain[None, :] * signal_wide
    gated = (readout * jax.nn.silu(gate_z.astype(F32))).astype(BF16)

    dense = lax.optimization_barrier(gated).reshape(16, own_rows * inner_dev // 16)
    same = spread(dense, RING, 16).reshape(16, own_rows, inner_dev)
    same = lax.optimization_barrier(same)
    other = swap(same, "c")
    rows = jnp.concatenate(
        [jnp.where(core == 0, same, other), jnp.where(core == 0, other, same)], axis=1
    )
    out_terms = dot(rows.reshape(16 * token_rows, inner_dev), out_weight).astype(BF16)
    out_own = jnp.sum(
        lax.all_to_all(out_terms.reshape(16, token_rows, token_cols), TENSOR, 0, 0).astype(F32),
        axis=0,
    )
    residual = (tokens.astype(F32) + out_own).astype(BF16)

    block = jnp.pad(residual, ((0, 8), (0, 0)))[None]
    sums = reduce_rows(block, token_rows, post_gain, gate_weight, up_weight, PAIRS)[0]
    scale = lax.rsqrt(sums[token_rows, :token_rows] / WIDTH + epsilon)[:, None]
    hidden = gate_weight.shape[1] // 2
    both = sums[:token_rows] * scale
    active = (jax.nn.silu(both[:, :hidden]) * both[:, hidden:]).astype(BF16)
    near = spread(active, PAIRS, 8)
    next_to = swap(near, "zp")
    same = jnp.concatenate(
        [jnp.where(pair == 0, near, next_to), jnp.where(pair == 0, next_to, near)], axis=0
    )
    other = swap(same, "c")
    same = same.reshape(16 * token_rows, hidden)
    other = other.reshape(16 * token_rows, hidden)
    down_terms = dot(same, half_rows(down_weight, core)) + dot(
        other, half_rows(down_weight, 1 - core)
    )
    down_own = jnp.sum(
        lax.all_to_all(
            down_terms.astype(BF16).reshape(16, token_rows, token_cols), TENSOR_PAIRS, 0, 0
        ).astype(F32),
        axis=0,
    )
    mixed = (residual.astype(F32) + down_own).astype(BF16)
    return (mixed, window[1:], new_state)


def solution(mesh):
    fine = Mesh(
        np.asarray(mesh.devices).reshape(4, 2, 2, 2, 4, 2, 2),
        ("zh", "zm", "zp", "c", "y", "xm", "xp"),
    )
    batch, tensor = ("zh", "zm", "zp", "c"), TENSOR
    return jax.shard_map(
        on_device,
        mesh=fine,
        in_specs=(
            P(tensor, batch),
            P(batch),
            P(batch, tensor),
            P(batch, tensor),
            P(None, batch, tensor),
            P(None, tensor),
            P(tensor),
            P(tensor, None),
            P(None, tensor),
            P(tensor),
            P(None, tensor),
            P(batch, None, tensor),
            P(tensor),
            P(tensor, batch),
            P(batch),
            P(batch, tensor),
            P(batch, tensor),
            P(tensor, batch),
        ),
        out_specs=(P(tensor, batch), P(None, batch, tensor), P(batch, None, tensor)),
        check_vma=False,
    )
```

```python
import jax
import jax.numpy as jnp
import numpy as np
from jax import lax
from jax.sharding import Mesh, PartitionSpec as P

WIDTH = 8192
RANK = 512
STATE = 16

epsilon = 1e-06

F32 = jnp.float32
BF16 = jnp.bfloat16
TENSOR = ("y", "xm", "xp")
TENSOR_PAIRS = ("xp", "y", "xm")
RING = ("zh", "zm", "zp")
PAIRS = ("zh", "zm")


def spread(block, axes, count):
    return lax.all_to_all(jnp.broadcast_to(block[None], (count,) + block.shape), axes, 0, 0)


def swap(block, axis):
    return lax.ppermute(block, axis, [(0, 1), (1, 0)])


def swap_pairs(block):
    moves = []
    for z in range(16):
        step = 1 if z % 2 == 0 else -1
        moves.append((2 * z, 2 * (z + step)))
        moves.append((2 * z + 1, 2 * ((z - step) % 16) + 1))
    return lax.ppermute(block, RING + ("c",), moves)


def dot(left, right):
    return jnp.dot(left, right, preferred_element_type=F32)


def add(left, right):
    return (left.astype(F32) + right.astype(F32)).astype(BF16)


def half_columns(weight, which):
    half = weight.shape[1] // 2
    return lax.dynamic_slice_in_dim(weight, which * half, half, 1)


def half_rows(block, which):
    half = block.shape[0] // 2
    return lax.dynamic_slice_in_dim(block, which * half, half, 0)


def reduce_rows(block, size, gain, left_weight, right_weight, axes):
    core, pair = lax.axis_index("c"), lax.axis_index("zp")
    groups, padded, depth = block.shape
    rows = spread(block.reshape(groups * padded, depth), TENSOR_PAIRS, 16)
    low, high = rows[:8], rows[8:]
    rows = jnp.concatenate(
        [jnp.where(pair == 0, high, low), jnp.where(pair == 0, low, high)], axis=0
    )
    wide = rows.astype(F32)
    scaled = (wide * gain[None, None, :]).astype(BF16).reshape(16 * groups * padded, depth)
    squares = jnp.sum(wide * wide, axis=2).reshape(16 * groups, 1, padded)
    half = left_weight.shape[1] // 2
    columns = half + half
    marks = jnp.pad(squares.astype(BF16), ((0, 0), (0, 0), (0, columns - padded)))
    spare = lax.broadcasted_iota(jnp.int32, (1, padded, columns), 1) == size

    def partial(which):
        weight = jnp.concatenate(
            [half_columns(left_weight, which), half_columns(right_weight, which)], axis=1
        )
        return jnp.where(
            spare, marks, dot(scaled, weight).astype(BF16).reshape(16 * groups, padded, columns)
        )

    received = swap(partial(1 - core), "c")
    both = add(partial(core), received)
    total = add(both[8 * groups :], swap_pairs(both[: 8 * groups]))
    far = lax.all_to_all(total, axes, 0, 0).astype(F32)
    return jnp.sum(far.reshape(8, groups, padded, columns), axis=0)


def on_device(
    tokens,
    norm_gain,
    in_x_weight,
    in_z_weight,
    conv_state,
    conv_weight,
    conv_bias,
    proj_weight,
    delta_weight,
    delta_bias,
    decay_log,
    ssm_state,
    skip_gain,
    out_weight,
    post_gain,
    gate_weight,
    up_weight,
    down_weight,
):
    core, pair = lax.axis_index("c"), lax.axis_index("zp")
    inner_dev = in_x_weight.shape[1]
    half = inner_dev // 2
    own_rows = conv_state.shape[1]
    token_rows, token_cols = tokens.shape

    block = jnp.pad(tokens.reshape(2, own_rows, token_cols), ((0, 0), (0, 4), (0, 0)))
    sums = reduce_rows(
        block, own_rows, norm_gain, in_x_weight, in_z_weight, ("zh", "zm", "c")
    )
    scale = lax.rsqrt(sums[0, own_rows, :own_rows] / WIDTH + epsilon)[:, None]
    mixed_in = (sums[:, :own_rows] * scale[None]).astype(BF16)
    inner_x = jnp.concatenate([mixed_in[0, :, :half], mixed_in[1, :, :half]], axis=1)
    gate_z = jnp.concatenate([mixed_in[0, :, half:], mixed_in[1, :, half:]], axis=1)
    window = jnp.concatenate([conv_state, inner_x[None]], axis=0)
    conv_pre = jnp.sum(window.astype(F32) * conv_weight[:, None, :], axis=0) + conv_bias[None, :]
    signal = jax.nn.silu(conv_pre).astype(BF16)
    projected = jnp.sum(
        spread(dot(signal, proj_weight).astype(BF16), TENSOR, 16).astype(F32), axis=0
    )
    delta_low = projected[:, :RANK]
    input_map = projected[:, RANK : RANK + STATE]
    output_map = projected[:, RANK + STATE :]
    delta_scale = lax.rsqrt(jnp.mean(delta_low * delta_low, axis=1, keepdims=True) + epsilon)
    delta_norm = (delta_low * delta_scale).astype(BF16)
    delta = jax.nn.softplus(dot(delta_norm, delta_weight) + delta_bias[None, :])
    signal_wide = signal.astype(F32)
    decay = jnp.exp(delta[:, None, :] * (-jnp.exp(decay_log))[None, :, :])
    new_state = decay * ssm_state + (delta * signal_wide)[:, None, :] * input_map[:, :, None]
    readout = jnp.sum(new_state * output_map[:, :, None], axis=1) + skip_gain[None, :] * signal_wide
    gated = (readout * jax.nn.silu(gate_z.astype(F32))).astype(BF16)

    dense = lax.optimization_barrier(gated).reshape(16, own_rows * inner_dev // 16)
    same = spread(dense, RING, 16).reshape(16, own_rows, inner_dev)
    same = lax.optimization_barrier(same)
    other = swap(same, "c")
    rows = jnp.concatenate(
        [jnp.where(core == 0, same, other), jnp.where(core == 0, other, same)], axis=1
    )
    out_terms = dot(rows.reshape(16 * token_rows, inner_dev), out_weight).astype(BF16)
    out_own = jnp.sum(
        lax.all_to_all(out_terms.reshape(16, token_rows, token_cols), TENSOR, 0, 0).astype(F32),
        axis=0,
    )
    residual = (tokens.astype(F32) + out_own).astype(BF16)

    block = jnp.pad(residual, ((0, 8), (0, 0)))[None]
    sums = reduce_rows(block, token_rows, post_gain, gate_weight, up_weight, PAIRS)[0]
    scale = lax.rsqrt(sums[token_rows, :token_rows] / WIDTH + epsilon)[:, None]
    hidden = gate_weight.shape[1] // 2
    both = sums[:token_rows] * scale
    active = (jax.nn.silu(both[:, :hidden]) * both[:, hidden:]).astype(BF16)
    near = spread(active, PAIRS, 8)
    next_to = swap_pairs(near)
    same = jnp.concatenate(
        [jnp.where(pair == 0, near, next_to), jnp.where(pair == 0, next_to, near)], axis=0
    )
    other = swap(same, "c")
    same = same.reshape(16 * token_rows, hidden)
    other = other.reshape(16 * token_rows, hidden)
    down_terms = dot(same, half_rows(down_weight, core)) + dot(
        other, half_rows(down_weight, 1 - core)
    )
    down_own = jnp.sum(
        lax.all_to_all(
            down_terms.astype(BF16).reshape(16, token_rows, token_cols), TENSOR_PAIRS, 0, 0
        ).astype(F32),
        axis=0,
    )
    mixed = (residual.astype(F32) + down_own).astype(BF16)
    return (mixed, window[1:], new_state)


def solution(mesh):
    fine = Mesh(
        np.asarray(mesh.devices).reshape(4, 2, 2, 2, 4, 2, 2),
        ("zh", "zm", "zp", "c", "y", "xm", "xp"),
    )
    batch, tensor = ("zh", "zm", "zp", "c"), TENSOR
    return jax.shard_map(
        on_device,
        mesh=fine,
        in_specs=(
            P(tensor, batch),
            P(batch),
            P(batch, tensor),
            P(batch, tensor),
            P(None, batch, tensor),
            P(None, tensor),
            P(tensor),
            P(tensor, None),
            P(None, tensor),
            P(tensor),
            P(None, tensor),
            P(batch, None, tensor),
            P(tensor),
            P(tensor, batch),
            P(batch),
            P(batch, tensor),
            P(batch, tensor),
            P(tensor, batch),
        ),
        out_specs=(P(tensor, batch), P(None, batch, tensor), P(batch, None, tensor)),
        check_vma=False,
    )
```

```python
import jax
import jax.numpy as jnp
import numpy as np
from jax import lax
from jax.sharding import Mesh, PartitionSpec as P

WIDTH = 8192
RANK = 512
STATE = 16
TILE = 256

epsilon = 1e-06

F32 = jnp.float32
BF16 = jnp.bfloat16
TENSOR = ("y", "xm", "xp")
TENSOR_PAIRS = ("xp", "y", "xm")
RING = ("zh", "zm", "zp")
PAIRS = ("zh", "zm")


def spread(block, axes, count):
    return lax.all_to_all(jnp.broadcast_to(block[None], (count,) + block.shape), axes, 0, 0)


def swap(block, axis):
    return lax.ppermute(block, axis, [(0, 1), (1, 0)])


def swap_pairs(block):
    moves = []
    for z in range(16):
        step = 1 if z % 2 == 0 else -1
        moves.append((2 * z, 2 * (z + step)))
        moves.append((2 * z + 1, 2 * ((z - step) % 16) + 1))
    return lax.ppermute(block, RING + ("c",), moves)


def dot(left, right):
    return jnp.dot(left, right, preferred_element_type=F32)


def add(left, right):
    return (left.astype(F32) + right.astype(F32)).astype(BF16)


def half_columns(weight, which):
    half = weight.shape[1] // 2
    return lax.dynamic_slice_in_dim(weight, which * half, half, 1)


def half_rows(block, which):
    half = block.shape[0] // 2
    return lax.dynamic_slice_in_dim(block, which * half, half, 0)


def reduce_rows(block, size, gain, left_weight, right_weight, axes):
    core, pair = lax.axis_index("c"), lax.axis_index("zp")
    groups, padded, depth = block.shape
    rows = spread(block.reshape(groups * padded, depth), TENSOR_PAIRS, 16)
    low, high = rows[:8], rows[8:]
    rows = jnp.concatenate(
        [jnp.where(pair == 0, high, low), jnp.where(pair == 0, low, high)], axis=0
    )
    wide = rows.astype(F32)
    scaled = (wide * gain[None, None, :]).astype(BF16).reshape(16 * groups * padded, depth)
    squares = jnp.sum(wide * wide, axis=2).reshape(16 * groups, 1, padded)
    half = left_weight.shape[1] // 2
    columns = half + half
    marks = jnp.pad(squares.astype(BF16), ((0, 0), (0, 0), (0, columns - padded)))
    spare = lax.broadcasted_iota(jnp.int32, (1, padded, columns), 1) == size

    def partial(which):
        weight = jnp.concatenate(
            [half_columns(left_weight, which), half_columns(right_weight, which)], axis=1
        )
        return jnp.where(
            spare, marks, dot(scaled, weight).astype(BF16).reshape(16 * groups, padded, columns)
        )

    received = swap(partial(1 - core), "c")
    both = add(partial(core), received)
    total = add(both[8 * groups :], swap_pairs(both[: 8 * groups]))
    far = lax.all_to_all(total, axes, 0, 0).astype(F32)
    return jnp.sum(far.reshape(8, groups, padded, columns), axis=0)


def reduce_wide_rows(block, gain, left_weight, right_weight):
    core, pair = lax.axis_index("c"), lax.axis_index("zp")
    size, depth = block.shape
    rows = spread(block, TENSOR_PAIRS, 16)
    low, high = rows[:8], rows[8:]
    rows = jnp.concatenate(
        [jnp.where(pair == 0, high, low), jnp.where(pair == 0, low, high)], axis=0
    )
    wide = rows.astype(F32)
    scaled = (wide * gain[None, None, :]).astype(BF16).reshape(16 * size, depth)
    squares = jnp.sum(wide * wide, axis=2).astype(BF16)[:, None, :]
    marks = jnp.pad(squares, ((0, 0), (0, 7), (0, TILE - size)))
    tiles = left_weight.shape[1] // TILE

    def partial(which):
        weight = jnp.concatenate(
            [half_columns(left_weight, which), half_columns(right_weight, which)], axis=1
        )
        terms = dot(scaled, weight).astype(BF16).reshape(16, size, tiles * TILE)
        return jnp.concatenate(
            [terms[:, :, TILE * k : TILE * k + TILE] for k in range(tiles)] + [marks], axis=1
        )

    received = swap(partial(1 - core), "c")
    both = add(partial(core), received)
    total = add(both[8:], swap_pairs(both[:8]))
    sums = jnp.sum(lax.all_to_all(total, PAIRS, 0, 0).astype(F32), axis=0)
    columns = [sums[size * k : size * k + size] for k in range(tiles)]
    return jnp.concatenate(columns, axis=1), sums[size * tiles, :size]


def on_device(
    tokens,
    norm_gain,
    in_x_weight,
    in_z_weight,
    conv_state,
    conv_weight,
    conv_bias,
    proj_weight,
    delta_weight,
    delta_bias,
    decay_log,
    ssm_state,
    skip_gain,
    out_weight,
    post_gain,
    gate_weight,
    up_weight,
    down_weight,
):
    core, pair = lax.axis_index("c"), lax.axis_index("zp")
    inner_dev = in_x_weight.shape[1]
    half = inner_dev // 2
    own_rows = conv_state.shape[1]
    token_rows, token_cols = tokens.shape

    block = jnp.pad(tokens.reshape(2, own_rows, token_cols), ((0, 0), (0, 4), (0, 0)))
    sums = reduce_rows(
        block, own_rows, norm_gain, in_x_weight, in_z_weight, ("zh", "zm", "c")
    )
    scale = lax.rsqrt(sums[0, own_rows, :own_rows] / WIDTH + epsilon)[:, None]
    mixed_in = (sums[:, :own_rows] * scale[None]).astype(BF16)
    inner_x = jnp.concatenate([mixed_in[0, :, :half], mixed_in[1, :, :half]], axis=1)
    gate_z = jnp.concatenate([mixed_in[0, :, half:], mixed_in[1, :, half:]], axis=1)
    window = jnp.concatenate([conv_state, inner_x[None]], axis=0)
    conv_pre = jnp.sum(window.astype(F32) * conv_weight[:, None, :], axis=0) + conv_bias[None, :]
    signal = jax.nn.silu(conv_pre).astype(BF16)
    projected = jnp.sum(
        spread(dot(signal, proj_weight).astype(BF16), TENSOR, 16).astype(F32), axis=0
    )
    delta_low = projected[:, :RANK]
    input_map = projected[:, RANK : RANK + STATE]
    output_map = projected[:, RANK + STATE :]
    delta_scale = lax.rsqrt(jnp.mean(delta_low * delta_low, axis=1, keepdims=True) + epsilon)
    delta_norm = (delta_low * delta_scale).astype(BF16)
    delta = jax.nn.softplus(dot(delta_norm, delta_weight) + delta_bias[None, :])
    signal_wide = signal.astype(F32)
    decay = jnp.exp(delta[:, None, :] * (-jnp.exp(decay_log))[None, :, :])
    new_state = decay * ssm_state + (delta * signal_wide)[:, None, :] * input_map[:, :, None]
    readout = jnp.sum(new_state * output_map[:, :, None], axis=1) + skip_gain[None, :] * signal_wide
    gated = (readout * jax.nn.silu(gate_z.astype(F32))).astype(BF16)

    dense = lax.optimization_barrier(gated).reshape(16, own_rows * inner_dev // 16)
    same = spread(dense, RING, 16).reshape(16, own_rows, inner_dev)
    same = lax.optimization_barrier(same)
    other = swap(same, "c")
    rows = jnp.concatenate(
        [jnp.where(core == 0, same, other), jnp.where(core == 0, other, same)], axis=1
    )
    out_terms = dot(rows.reshape(16 * token_rows, inner_dev), out_weight).astype(BF16)
    out_own = jnp.sum(
        lax.all_to_all(out_terms.reshape(16, token_rows, token_cols), TENSOR, 0, 0).astype(F32),
        axis=0,
    )
    residual = (tokens.astype(F32) + out_own).astype(BF16)

    sums, second = reduce_wide_rows(residual, post_gain, gate_weight, up_weight)
    scale = lax.rsqrt(second / WIDTH + epsilon)[:, None]
    hidden = gate_weight.shape[1] // 2
    both = sums * scale
    active = (jax.nn.silu(both[:, :hidden]) * both[:, hidden:]).astype(BF16)
    near = spread(active, PAIRS, 8)
    next_to = swap_pairs(near)
    same = jnp.concatenate(
        [jnp.where(pair == 0, near, next_to), jnp.where(pair == 0, next_to, near)], axis=0
    )
    other = swap(same, "c")
    same = same.reshape(16 * token_rows, hidden)
    other = other.reshape(16 * token_rows, hidden)
    down_terms = dot(same, half_rows(down_weight, core)) + dot(
        other, half_rows(down_weight, 1 - core)
    )
    down_own = jnp.sum(
        lax.all_to_all(
            down_terms.astype(BF16).reshape(16, token_rows, token_cols), TENSOR_PAIRS, 0, 0
        ).astype(F32),
        axis=0,
    )
    mixed = (residual.astype(F32) + down_own).astype(BF16)
    return (mixed, window[1:], new_state)


def solution(mesh):
    fine = Mesh(
        np.asarray(mesh.devices).reshape(4, 2, 2, 2, 4, 2, 2),
        ("zh", "zm", "zp", "c", "y", "xm", "xp"),
    )
    batch, tensor = ("zh", "zm", "zp", "c"), TENSOR
    return jax.shard_map(
        on_device,
        mesh=fine,
        in_specs=(
            P(tensor, batch),
            P(batch),
            P(batch, tensor),
            P(batch, tensor),
            P(None, batch, tensor),
            P(None, tensor),
            P(tensor),
            P(tensor, None),
            P(None, tensor),
            P(tensor),
            P(None, tensor),
            P(batch, None, tensor),
            P(tensor),
            P(tensor, batch),
            P(batch),
            P(batch, tensor),
            P(batch, tensor),
            P(tensor, batch),
        ),
        out_specs=(P(tensor, batch), P(None, batch, tensor), P(batch, None, tensor)),
        check_vma=False,
    )
```

```python
import jax
import jax.numpy as jnp
import numpy as np
from jax import lax
from jax.sharding import Mesh, PartitionSpec as P

WIDTH = 8192
RANK = 512
STATE = 16
TILE = 256

epsilon = 1e-06

F32 = jnp.float32
BF16 = jnp.bfloat16
TENSOR = ("y", "xm", "xp")
TENSOR_PAIRS = ("xp", "y", "xm")
RING = ("zh", "zm", "zp")
PAIRS = ("zh", "zm")


def spread(block, axes, count):
    return lax.all_to_all(jnp.broadcast_to(block[None], (count,) + block.shape), axes, 0, 0)


def swap(block, axis):
    return lax.ppermute(block, axis, [(0, 1), (1, 0)])


def swap_pairs(block):
    moves = []
    for z in range(16):
        step = 1 if z % 2 == 0 else -1
        moves.append((2 * z, 2 * (z + step)))
        moves.append((2 * z + 1, 2 * ((z - step) % 16) + 1))
    return lax.ppermute(block, RING + ("c",), moves)


def dot(left, right):
    return jnp.dot(left, right, preferred_element_type=F32)


def add(left, right):
    return (left.astype(F32) + right.astype(F32)).astype(BF16)


def half_columns(weight, which):
    half = weight.shape[1] // 2
    return lax.dynamic_slice_in_dim(weight, which * half, half, 1)


def half_rows(block, which):
    half = block.shape[0] // 2
    return lax.dynamic_slice_in_dim(block, which * half, half, 0)


def spread_rows(block):
    rows = spread(block, TENSOR_PAIRS, 16)
    low, high = rows[:8], rows[8:]
    even = lax.axis_index("zp") == 0
    return jnp.concatenate([jnp.where(even, high, low), jnp.where(even, low, high)], axis=0)


def reduce_rows(block, gain, weight):
    first_core = lax.axis_index("c") == 0
    rows = spread_rows(block)
    size = rows.shape[1] // 2
    columns = weight.shape[1]
    padded = size + 4
    spare = lax.broadcasted_iota(jnp.int32, (1, padded, columns), 1) == size
    low, high = rows[:, :size], rows[:, size:]

    def partial(part):
        wide = jnp.pad(part, ((0, 0), (0, 4), (0, 0))).astype(F32)
        scaled = (wide * gain[None, None, :]).astype(BF16).reshape(16 * padded, -1)
        squares = jnp.sum(wide * wide, axis=2).astype(BF16)[:, None, :]
        marks = jnp.pad(squares, ((0, 0), (0, 0), (0, columns - padded)))
        return jnp.where(spare, marks, dot(scaled, weight).astype(BF16).reshape(16, padded, columns))

    received = swap(partial(jnp.where(first_core, high, low)), "c")
    both = add(partial(jnp.where(first_core, low, high)), received)
    total = add(both[8:], swap_pairs(both[:8]))
    sums = jnp.sum(lax.all_to_all(total, PAIRS, 0, 0).astype(F32), axis=0)
    return sums[:size], sums[size, :size]


def reduce_wide_rows(block, gain, left_weight, right_weight):
    core = lax.axis_index("c")
    size, depth = block.shape
    rows = spread_rows(block)
    wide = rows.astype(F32)
    scaled = (wide * gain[None, None, :]).astype(BF16).reshape(16 * size, depth)
    squares = jnp.sum(wide * wide, axis=2).astype(BF16)[:, None, :]
    marks = jnp.pad(squares, ((0, 0), (0, 7), (0, TILE - size)))
    tiles = left_weight.shape[1] // TILE

    def partial(which):
        weight = jnp.concatenate(
            [half_columns(left_weight, which), half_columns(right_weight, which)], axis=1
        )
        terms = dot(scaled, weight).astype(BF16).reshape(16, size, tiles * TILE)
        return jnp.concatenate(
            [terms[:, :, TILE * k : TILE * k + TILE] for k in range(tiles)] + [marks], axis=1
        )

    received = swap(partial(1 - core), "c")
    both = add(partial(core), received)
    total = add(both[8:], swap_pairs(both[:8]))
    sums = jnp.sum(lax.all_to_all(total, PAIRS, 0, 0).astype(F32), axis=0)
    columns = [sums[size * k : size * k + size] for k in range(tiles)]
    return jnp.concatenate(columns, axis=1), sums[size * tiles, :size]


def on_device(
    tokens,
    norm_gain,
    in_x_weight,
    in_z_weight,
    conv_state,
    conv_weight,
    conv_bias,
    proj_weight,
    delta_weight,
    delta_bias,
    decay_log,
    ssm_state,
    skip_gain,
    out_weight,
    post_gain,
    gate_weight,
    up_weight,
    down_weight,
):
    core, pair = lax.axis_index("c"), lax.axis_index("zp")
    inner_dev = in_x_weight.shape[1]
    own_rows = conv_state.shape[1]
    token_rows, token_cols = tokens.shape

    sums, first = reduce_rows(
        tokens, norm_gain, jnp.concatenate([in_x_weight, in_z_weight], axis=1)
    )
    scale = lax.rsqrt(first / WIDTH + epsilon)[:, None]
    inner_x = (sums[:, :inner_dev] * scale).astype(BF16)
    gate_z = (sums[:, inner_dev:] * scale).astype(BF16)
    window = jnp.concatenate([conv_state, inner_x[None]], axis=0)
    conv_pre = jnp.sum(window.astype(F32) * conv_weight[:, None, :], axis=0) + conv_bias[None, :]
    signal = jax.nn.silu(conv_pre).astype(BF16)
    projected = jnp.sum(
        spread(dot(signal, proj_weight).astype(BF16), TENSOR, 16).astype(F32), axis=0
    )
    delta_low = projected[:, :RANK]
    input_map = projected[:, RANK : RANK + STATE]
    output_map = projected[:, RANK + STATE :]
    delta_scale = lax.rsqrt(jnp.mean(delta_low * delta_low, axis=1, keepdims=True) + epsilon)
    delta_norm = (delta_low * delta_scale).astype(BF16)
    delta = jax.nn.softplus(dot(delta_norm, delta_weight) + delta_bias[None, :])
    signal_wide = signal.astype(F32)
    decay = jnp.exp(delta[:, None, :] * (-jnp.exp(decay_log))[None, :, :])
    new_state = decay * ssm_state + (delta * signal_wide)[:, None, :] * input_map[:, :, None]
    readout = jnp.sum(new_state * output_map[:, :, None], axis=1) + skip_gain[None, :] * signal_wide
    gated = (readout * jax.nn.silu(gate_z.astype(F32))).astype(BF16)

    dense = lax.optimization_barrier(gated).reshape(16, own_rows * inner_dev // 16)
    same = spread(dense, RING, 16).reshape(16, own_rows, inner_dev)
    same = lax.optimization_barrier(same)
    other = swap(same, "c")
    rows = jnp.concatenate(
        [jnp.where(core == 0, same, other), jnp.where(core == 0, other, same)], axis=1
    )
    out_terms = dot(rows.reshape(16 * token_rows, inner_dev), out_weight).astype(BF16)
    out_own = jnp.sum(
        lax.all_to_all(out_terms.reshape(16, token_rows, token_cols), TENSOR, 0, 0).astype(F32),
        axis=0,
    )
    residual = (tokens.astype(F32) + out_own).astype(BF16)

    sums, second = reduce_wide_rows(residual, post_gain, gate_weight, up_weight)
    scale = lax.rsqrt(second / WIDTH + epsilon)[:, None]
    hidden = gate_weight.shape[1] // 2
    both = sums * scale
    active = (jax.nn.silu(both[:, :hidden]) * both[:, hidden:]).astype(BF16)
    near = spread(active, PAIRS, 8)
    next_to = swap_pairs(near)
    own_part, other_part = half_rows(down_weight, core), half_rows(down_weight, 1 - core)

    def down(same, other):
        flat = (8 * token_rows, hidden)
        return dot(same.reshape(flat), own_part) + dot(other.reshape(flat), other_part)

    near_terms = down(near, swap(near, "c"))
    next_terms = down(next_to, swap(next_to, "c"))
    down_terms = jnp.concatenate(
        [
            jnp.where(pair == 0, near_terms, next_terms),
            jnp.where(pair == 0, next_terms, near_terms),
        ],
        axis=0,
    )
    down_own = jnp.sum(
        lax.all_to_all(
            down_terms.astype(BF16).reshape(16, token_rows, token_cols), TENSOR_PAIRS, 0, 0
        ).astype(F32),
        axis=0,
    )
    mixed = (residual.astype(F32) + down_own).astype(BF16)
    return (mixed, window[1:], new_state)


def solution(mesh):
    fine = Mesh(
        np.asarray(mesh.devices).reshape(4, 2, 2, 2, 4, 2, 2),
        ("zh", "zm", "zp", "c", "y", "xm", "xp"),
    )
    batch, tensor = ("zh", "zm", "zp", "c"), TENSOR
    return jax.shard_map(
        on_device,
        mesh=fine,
        in_specs=(
            P(tensor, batch),
            P(batch),
            P(batch, tensor),
            P(batch, tensor),
            P(None, batch, tensor),
            P(None, tensor),
            P(tensor),
            P(tensor, None),
            P(None, tensor),
            P(tensor),
            P(None, tensor),
            P(batch, None, tensor),
            P(tensor),
            P(tensor, batch),
            P(batch),
            P(batch, tensor),
            P(batch, tensor),
            P(tensor, batch),
        ),
        out_specs=(P(tensor, batch), P(None, batch, tensor), P(batch, None, tensor)),
        check_vma=False,
    )
```

```python
import jax
import jax.numpy as jnp
import numpy as np
from jax import lax
from jax.sharding import Mesh, PartitionSpec as P

WIDTH = 8192
RANK = 512
STATE = 16
TILE = 256

epsilon = 1e-06

F32 = jnp.float32
BF16 = jnp.bfloat16
TENSOR = ("y", "xm", "xp")
RING = ("zh", "zm", "zp")
PAIRS = ("zh", "zm")


def spread(block, axes, count):
    return lax.all_to_all(jnp.broadcast_to(block[None], (count,) + block.shape), axes, 0, 0)


def planes(first):
    groups = []
    for plane in range(32):
        parity = (plane // 2) % 2 ^ first
        tensor = list(range(parity, 16, 2)) + list(range(1 - parity, 16, 2))
        groups.append([16 * plane + place for place in tensor])
    return groups


def exchange(blocks, first):
    return lax.all_to_all(blocks, RING + ("c",) + TENSOR, 0, 0, axis_index_groups=planes(first))


def swap(block, axis):
    return lax.ppermute(block, axis, [(0, 1), (1, 0)])


def swap_pairs(block):
    moves = []
    for z in range(16):
        step = 1 if z % 2 == 0 else -1
        moves.append((2 * z, 2 * (z + step)))
        moves.append((2 * z + 1, 2 * ((z - step) % 16) + 1))
    return lax.ppermute(block, RING + ("c",), moves)


def dot(left, right):
    return jnp.dot(left, right, preferred_element_type=F32)


def add(left, right):
    return (left.astype(F32) + right.astype(F32)).astype(BF16)


def half_columns(weight, which):
    half = weight.shape[1] // 2
    return lax.dynamic_slice_in_dim(weight, which * half, half, 1)


def half_rows(block, which):
    half = block.shape[0] // 2
    return lax.dynamic_slice_in_dim(block, which * half, half, 0)


def spread_rows(block):
    return exchange(jnp.broadcast_to(block[None], (16,) + block.shape), 1)


def reduce_rows(block, gain, weight):
    first_core = lax.axis_index("c") == 0
    rows = spread_rows(block)
    size = rows.shape[1] // 2
    columns = weight.shape[1]
    padded = size + 4
    spare = lax.broadcasted_iota(jnp.int32, (1, padded, columns), 1) == size
    low, high = rows[:, :size], rows[:, size:]

    def partial(part):
        wide = jnp.pad(part, ((0, 0), (0, 4), (0, 0))).astype(F32)
        scaled = (wide * gain[None, None, :]).astype(BF16).reshape(16 * padded, -1)
        squares = jnp.sum(wide * wide, axis=2).astype(BF16)[:, None, :]
        marks = jnp.pad(squares, ((0, 0), (0, 0), (0, columns - padded)))
        return jnp.where(spare, marks, dot(scaled, weight).astype(BF16).reshape(16, padded, columns))

    received = swap(partial(jnp.where(first_core, high, low)), "c")
    both = add(partial(jnp.where(first_core, low, high)), received)
    total = add(both[8:], swap_pairs(both[:8]))
    sums = jnp.sum(lax.all_to_all(total, PAIRS, 0, 0).astype(F32), axis=0)
    return sums[:size], sums[size, :size]


def reduce_wide_rows(block, gain, left_weight, right_weight):
    core = lax.axis_index("c")
    size, depth = block.shape
    rows = spread_rows(block)
    wide = rows.astype(F32)
    scaled = (wide * gain[None, None, :]).astype(BF16).reshape(16 * size, depth)
    squares = jnp.sum(wide * wide, axis=2).astype(BF16)[:, None, :]
    marks = jnp.pad(squares, ((0, 0), (0, 7), (0, TILE - size)))
    tiles = left_weight.shape[1] // TILE

    def partial(which):
        weight = jnp.concatenate(
            [half_columns(left_weight, which), half_columns(right_weight, which)], axis=1
        )
        terms = dot(scaled, weight).astype(BF16).reshape(16, size, tiles * TILE)
        return jnp.concatenate(
            [terms[:, :, TILE * k : TILE * k + TILE] for k in range(tiles)] + [marks], axis=1
        )

    received = swap(partial(1 - core), "c")
    both = add(partial(core), received)
    total = add(both[8:], swap_pairs(both[:8]))
    sums = jnp.sum(lax.all_to_all(total, PAIRS, 0, 0).astype(F32), axis=0)
    columns = [sums[size * k : size * k + size] for k in range(tiles)]
    return jnp.concatenate(columns, axis=1), sums[size * tiles, :size]


def on_device(
    tokens,
    norm_gain,
    in_x_weight,
    in_z_weight,
    conv_state,
    conv_weight,
    conv_bias,
    proj_weight,
    delta_weight,
    delta_bias,
    decay_log,
    ssm_state,
    skip_gain,
    out_weight,
    post_gain,
    gate_weight,
    up_weight,
    down_weight,
):
    core = lax.axis_index("c")
    inner_dev = in_x_weight.shape[1]
    own_rows = conv_state.shape[1]
    token_rows, token_cols = tokens.shape

    sums, first = reduce_rows(
        tokens, norm_gain, jnp.concatenate([in_x_weight, in_z_weight], axis=1)
    )
    scale = lax.rsqrt(first / WIDTH + epsilon)[:, None]
    inner_x = (sums[:, :inner_dev] * scale).astype(BF16)
    gate_z = (sums[:, inner_dev:] * scale).astype(BF16)
    window = jnp.concatenate([conv_state, inner_x[None]], axis=0)
    conv_pre = jnp.sum(window.astype(F32) * conv_weight[:, None, :], axis=0) + conv_bias[None, :]
    signal = jax.nn.silu(conv_pre).astype(BF16)
    projected = jnp.sum(
        spread(dot(signal, proj_weight).astype(BF16), TENSOR, 16).astype(F32), axis=0
    )
    delta_low = projected[:, :RANK]
    input_map = projected[:, RANK : RANK + STATE]
    output_map = projected[:, RANK + STATE :]
    delta_scale = lax.rsqrt(jnp.mean(delta_low * delta_low, axis=1, keepdims=True) + epsilon)
    delta_norm = (delta_low * delta_scale).astype(BF16)
    delta = jax.nn.softplus(dot(delta_norm, delta_weight) + delta_bias[None, :])
    signal_wide = signal.astype(F32)
    decay = jnp.exp(delta[:, None, :] * (-jnp.exp(decay_log))[None, :, :])
    new_state = decay * ssm_state + (delta * signal_wide)[:, None, :] * input_map[:, :, None]
    readout = jnp.sum(new_state * output_map[:, :, None], axis=1) + skip_gain[None, :] * signal_wide
    gated = (readout * jax.nn.silu(gate_z.astype(F32))).astype(BF16)

    dense = lax.optimization_barrier(gated).reshape(16, own_rows * inner_dev // 16)
    same = spread(dense, RING, 16).reshape(16, own_rows, inner_dev)
    same = lax.optimization_barrier(same)
    other = swap(same, "c")
    rows = jnp.concatenate(
        [jnp.where(core == 0, same, other), jnp.where(core == 0, other, same)], axis=1
    )
    out_terms = dot(rows.reshape(16 * token_rows, inner_dev), out_weight).astype(BF16)
    out_own = jnp.sum(
        lax.all_to_all(out_terms.reshape(16, token_rows, token_cols), TENSOR, 0, 0).astype(F32),
        axis=0,
    )
    residual = (tokens.astype(F32) + out_own).astype(BF16)

    sums, second = reduce_wide_rows(residual, post_gain, gate_weight, up_weight)
    scale = lax.rsqrt(second / WIDTH + epsilon)[:, None]
    hidden = gate_weight.shape[1] // 2
    both = sums * scale
    active = (jax.nn.silu(both[:, :hidden]) * both[:, hidden:]).astype(BF16)
    near = spread(active, PAIRS, 8)
    next_to = swap_pairs(near)
    own_part, other_part = half_rows(down_weight, core), half_rows(down_weight, 1 - core)

    def down(same, other):
        flat = (8 * token_rows, hidden)
        return dot(same.reshape(flat), own_part) + dot(other.reshape(flat), other_part)

    near_terms = down(near, swap(near, "c"))
    next_terms = down(next_to, swap(next_to, "c"))
    down_terms = jnp.concatenate([near_terms, next_terms], axis=0).astype(BF16)
    down_own = jnp.sum(
        exchange(down_terms.reshape(16, token_rows, token_cols), 0).astype(F32), axis=0
    )
    mixed = (residual.astype(F32) + down_own).astype(BF16)
    return (mixed, window[1:], new_state)


def solution(mesh):
    fine = Mesh(
        np.asarray(mesh.devices).reshape(4, 2, 2, 2, 4, 2, 2),
        ("zh", "zm", "zp", "c", "y", "xm", "xp"),
    )
    batch, tensor = ("zh", "zm", "zp", "c"), TENSOR
    return jax.shard_map(
        on_device,
        mesh=fine,
        in_specs=(
            P(tensor, batch),
            P(batch),
            P(batch, tensor),
            P(batch, tensor),
            P(None, batch, tensor),
            P(None, tensor),
            P(tensor),
            P(tensor, None),
            P(None, tensor),
            P(tensor),
            P(None, tensor),
            P(batch, None, tensor),
            P(tensor),
            P(tensor, batch),
            P(batch),
            P(batch, tensor),
            P(batch, tensor),
            P(tensor, batch),
        ),
        out_specs=(P(tensor, batch), P(None, batch, tensor), P(batch, None, tensor)),
        check_vma=False,
    )
```

```python
import jax
import jax.numpy as jnp
import numpy as np
from jax import lax
from jax.sharding import Mesh, PartitionSpec as P

WIDTH = 8192
RANK = 512
STATE = 16
TILE = 256

epsilon = 1e-06

F32 = jnp.float32
BF16 = jnp.bfloat16
TENSOR = ("y", "xm", "xp")
RING = ("zh", "zm", "zp")
PAIRS = ("zh", "zm")


def spread(block, axes, count):
    return lax.all_to_all(jnp.broadcast_to(block[None], (count,) + block.shape), axes, 0, 0)


def planes(first):
    groups = []
    for plane in range(32):
        parity = (plane // 2) % 2 ^ first
        tensor = list(range(parity, 16, 2)) + list(range(1 - parity, 16, 2))
        groups.append([16 * plane + place for place in tensor])
    return groups


def exchange(blocks, first):
    return lax.all_to_all(blocks, RING + ("c",) + TENSOR, 0, 0, axis_index_groups=planes(first))


def swap(block, axis):
    return lax.ppermute(block, axis, [(0, 1), (1, 0)])


def swap_pairs(block):
    moves = []
    for z in range(16):
        step = 1 if z % 2 == 0 else -1
        moves.append((2 * z, 2 * (z + step)))
        moves.append((2 * z + 1, 2 * ((z - step) % 16) + 1))
    return lax.ppermute(block, RING + ("c",), moves)


def dot(left, right):
    return jnp.dot(left, right, preferred_element_type=F32)


def add(left, right):
    return (left.astype(F32) + right.astype(F32)).astype(BF16)


def half_columns(weight, which):
    half = weight.shape[1] // 2
    return lax.dynamic_slice_in_dim(weight, which * half, half, 1)


def half_rows(block, which):
    half = block.shape[0] // 2
    return lax.dynamic_slice_in_dim(block, which * half, half, 0)


def spread_rows(block):
    return exchange(jnp.broadcast_to(block[None], (16,) + block.shape), 1)


def reduce_rows(block, gain, weight):
    first_core = lax.axis_index("c") == 0
    rows = spread_rows(block)
    size = rows.shape[1] // 2
    columns = weight.shape[1]
    padded = size + 4
    spare = lax.broadcasted_iota(jnp.int32, (1, padded, columns), 1) == size
    low, high = rows[:, :size], rows[:, size:]

    def partial(part):
        wide = jnp.pad(part, ((0, 0), (0, 4), (0, 0))).astype(F32)
        scaled = (wide * gain[None, None, :]).astype(BF16).reshape(16 * padded, -1)
        squares = jnp.sum(wide * wide, axis=2).astype(BF16)[:, None, :]
        marks = jnp.pad(squares, ((0, 0), (0, 0), (0, columns - padded)))
        return jnp.where(spare, marks, dot(scaled, weight).astype(BF16).reshape(16, padded, columns))

    received = swap(partial(jnp.where(first_core, high, low)), "c")
    both = add(partial(jnp.where(first_core, low, high)), received)
    total = add(both[8:], swap_pairs(both[:8]))
    sums = jnp.sum(lax.all_to_all(total, PAIRS, 0, 0).astype(F32), axis=0)
    return sums[:size], sums[size, :size]


def reduce_wide_rows(block, gain, left_weight, right_weight):
    core = lax.axis_index("c")
    size, depth = block.shape
    rows = spread_rows(block)
    wide = rows.astype(F32)
    scaled = (wide * gain[None, None, :]).astype(BF16).reshape(16 * size, depth)
    squares = jnp.sum(wide * wide, axis=2).astype(BF16)[:, None, :]
    marks = jnp.pad(squares, ((0, 0), (0, 7), (0, TILE - size)))
    tiles = left_weight.shape[1] // TILE

    def partial(which):
        weight = jnp.concatenate(
            [half_columns(left_weight, which), half_columns(right_weight, which)], axis=1
        )
        terms = dot(scaled, weight).astype(BF16).reshape(16, size, tiles * TILE)
        return jnp.concatenate(
            [terms[:, :, TILE * k : TILE * k + TILE] for k in range(tiles)] + [marks], axis=1
        )

    received = swap(partial(1 - core), "c")
    both = add(partial(core), received)
    total = add(both[8:], swap_pairs(both[:8]))
    sums = jnp.sum(lax.all_to_all(total, PAIRS, 0, 0).astype(F32), axis=0)
    columns = [sums[size * k : size * k + size] for k in range(tiles)]
    return jnp.concatenate(columns, axis=1), sums[size * tiles, :size]


def on_device(
    tokens,
    norm_gain,
    in_x_weight,
    in_z_weight,
    conv_state,
    conv_weight,
    conv_bias,
    proj_weight,
    delta_weight,
    delta_bias,
    decay_log,
    ssm_state,
    skip_gain,
    out_weight,
    post_gain,
    gate_weight,
    up_weight,
    down_weight,
):
    core = lax.axis_index("c")
    inner_dev = in_x_weight.shape[1]
    own_rows = conv_state.shape[1]
    token_rows, token_cols = tokens.shape

    sums, first = reduce_rows(
        tokens, norm_gain, jnp.concatenate([in_x_weight, in_z_weight], axis=1)
    )
    scale = lax.rsqrt(first / WIDTH + epsilon)[:, None]
    inner_x = (sums[:, :inner_dev] * scale).astype(BF16)
    gate_z = (sums[:, inner_dev:] * scale).astype(BF16)
    window = jnp.concatenate([conv_state, inner_x[None]], axis=0)
    conv_pre = jnp.sum(window.astype(F32) * conv_weight[:, None, :], axis=0) + conv_bias[None, :]
    signal = jax.nn.silu(conv_pre).astype(BF16)
    projected = jnp.sum(
        spread(dot(signal, proj_weight).astype(BF16), TENSOR, 16).astype(F32), axis=0
    )
    delta_low = projected[:, :RANK]
    input_map = projected[:, RANK : RANK + STATE]
    output_map = projected[:, RANK + STATE :]
    delta_scale = lax.rsqrt(jnp.mean(delta_low * delta_low, axis=1, keepdims=True) + epsilon)
    delta_norm = (delta_low * delta_scale).astype(BF16)
    delta = jax.nn.softplus(dot(delta_norm, delta_weight) + delta_bias[None, :])
    signal_wide = signal.astype(F32)
    decay = jnp.exp(delta[:, None, :] * (-jnp.exp(decay_log))[None, :, :])
    new_state = decay * ssm_state + (delta * signal_wide)[:, None, :] * input_map[:, :, None]
    readout = jnp.sum(new_state * output_map[:, :, None], axis=1) + skip_gain[None, :] * signal_wide
    gated = (readout * jax.nn.silu(gate_z.astype(F32))).astype(BF16)

    dense = lax.optimization_barrier(gated).reshape(16, own_rows * inner_dev // 16)
    near = spread(dense, PAIRS, 8).reshape(8, own_rows, inner_dev)
    near = lax.optimization_barrier(near)

    def out(same):
        rows = jnp.concatenate([same, swap(same, "c")], axis=1)
        return dot(rows.reshape(8 * token_rows, inner_dev), out_weight).astype(BF16)

    next_to = swap_pairs(near)
    out_terms = jnp.concatenate([out(near), out(next_to)], axis=0)
    out_sum = jnp.sum(
        exchange(out_terms.reshape(16, token_rows, token_cols), 0).astype(F32), axis=0
    )
    turned = jnp.concatenate([out_sum[own_rows:], out_sum[:own_rows]], axis=0)
    out_own = jnp.where(core == 0, out_sum, turned)
    residual = (tokens.astype(F32) + out_own).astype(BF16)

    sums, second = reduce_wide_rows(residual, post_gain, gate_weight, up_weight)
    scale = lax.rsqrt(second / WIDTH + epsilon)[:, None]
    hidden = gate_weight.shape[1] // 2
    both = sums * scale
    active = (jax.nn.silu(both[:, :hidden]) * both[:, hidden:]).astype(BF16)
    near = spread(active, PAIRS, 8)
    next_to = swap_pairs(near)
    own_part, other_part = half_rows(down_weight, core), half_rows(down_weight, 1 - core)

    def down(same, other):
        flat = (8 * token_rows, hidden)
        return dot(same.reshape(flat), own_part) + dot(other.reshape(flat), other_part)

    near_terms = down(near, swap(near, "c"))
    next_terms = down(next_to, swap(next_to, "c"))
    down_terms = jnp.concatenate([near_terms, next_terms], axis=0).astype(BF16)
    down_own = jnp.sum(
        exchange(down_terms.reshape(16, token_rows, token_cols), 0).astype(F32), axis=0
    )
    mixed = (residual.astype(F32) + down_own).astype(BF16)
    return (mixed, window[1:], new_state)


def solution(mesh):
    fine = Mesh(
        np.asarray(mesh.devices).reshape(4, 2, 2, 2, 4, 2, 2),
        ("zh", "zm", "zp", "c", "y", "xm", "xp"),
    )
    batch, tensor = ("zh", "zm", "zp", "c"), TENSOR
    return jax.shard_map(
        on_device,
        mesh=fine,
        in_specs=(
            P(tensor, batch),
            P(batch),
            P(batch, tensor),
            P(batch, tensor),
            P(None, batch, tensor),
            P(None, tensor),
            P(tensor),
            P(tensor, None),
            P(None, tensor),
            P(tensor),
            P(None, tensor),
            P(batch, None, tensor),
            P(tensor),
            P(tensor, batch),
            P(batch),
            P(batch, tensor),
            P(batch, tensor),
            P(tensor, batch),
        ),
        out_specs=(P(tensor, batch), P(None, batch, tensor), P(batch, None, tensor)),
        check_vma=False,
    )
```

```python
import jax
import jax.numpy as jnp
import numpy as np
from jax import lax
from jax.sharding import Mesh, PartitionSpec as P

WIDTH = 8192
RANK = 512
STATE = 16
TILE = 256

epsilon = 1e-06

F32 = jnp.float32
BF16 = jnp.bfloat16
TENSOR = ("y", "xm", "xp")
RING = ("zh", "zm", "zp")
PAIRS = ("zh", "zm")


def spread(block, axes, count):
    return lax.all_to_all(jnp.broadcast_to(block[None], (count,) + block.shape), axes, 0, 0)


def planes(first):
    groups = []
    for plane in range(32):
        parity = (plane // 2) % 2 ^ first
        tensor = list(range(parity, 16, 2)) + list(range(1 - parity, 16, 2))
        groups.append([16 * plane + place for place in tensor])
    return groups


def exchange(blocks, first):
    return lax.all_to_all(blocks, RING + ("c",) + TENSOR, 0, 0, axis_index_groups=planes(first))


def swap(block, axis):
    return lax.ppermute(block, axis, [(0, 1), (1, 0)])


def swap_pairs(block):
    moves = []
    for z in range(16):
        step = 1 if z % 2 == 0 else -1
        moves.append((2 * z, 2 * (z + step)))
        moves.append((2 * z + 1, 2 * ((z - step) % 16) + 1))
    return lax.ppermute(block, RING + ("c",), moves)


def dot(left, right):
    return jnp.dot(left, right, preferred_element_type=F32)


def add(left, right):
    return (left.astype(F32) + right.astype(F32)).astype(BF16)


def half_columns(weight, which):
    half = weight.shape[1] // 2
    return lax.dynamic_slice_in_dim(weight, which * half, half, 1)


def half_rows(block, which):
    half = block.shape[0] // 2
    return lax.dynamic_slice_in_dim(block, which * half, half, 0)


def spread_rows(block):
    return exchange(jnp.broadcast_to(block[None], (16,) + block.shape), 1)


def reduce_rows(block, gain, weight):
    first_core = lax.axis_index("c") == 0
    rows = spread_rows(block)
    size = rows.shape[1] // 2
    columns = weight.shape[1]
    padded = size + 4
    spare = lax.broadcasted_iota(jnp.int32, (1, padded, columns), 1) == size

    def partial(part):
        wide = jnp.pad(part, ((0, 0), (0, 4), (0, 0))).astype(F32)
        scaled = (wide * gain[None, None, :]).astype(BF16).reshape(8 * padded, -1)
        squares = jnp.sum(wide * wide, axis=2).astype(BF16)[:, None, :]
        marks = jnp.pad(squares, ((0, 0), (0, 0), (0, columns - padded)))
        return jnp.where(spare, marks, dot(scaled, weight).astype(BF16).reshape(8, padded, columns))

    def chip_sum(part):
        low, high = part[:, :size], part[:, size:]
        received = swap(partial(jnp.where(first_core, high, low)), "c")
        return add(partial(jnp.where(first_core, low, high)), received)

    met = swap_pairs(chip_sum(rows[:8]))
    total = add(chip_sum(rows[8:]), met)
    sums = jnp.sum(lax.all_to_all(total, PAIRS, 0, 0).astype(F32), axis=0)
    return sums[:size], sums[size, :size]


def reduce_wide_rows(block, gain, left_weight, right_weight):
    core = lax.axis_index("c")
    size, depth = block.shape
    rows = spread_rows(block)
    tiles = left_weight.shape[1] // TILE

    def chip_sum(part):
        wide = part.astype(F32)
        scaled = (wide * gain[None, None, :]).astype(BF16).reshape(8 * size, depth)
        squares = jnp.sum(wide * wide, axis=2).astype(BF16)[:, None, :]
        marks = jnp.pad(squares, ((0, 0), (0, 7), (0, TILE - size)))

        def partial(which):
            weight = jnp.concatenate(
                [half_columns(left_weight, which), half_columns(right_weight, which)], axis=1
            )
            terms = dot(scaled, weight).astype(BF16).reshape(8, size, tiles * TILE)
            return jnp.concatenate(
                [terms[:, :, TILE * k : TILE * k + TILE] for k in range(tiles)] + [marks], axis=1
            )

        received = swap(partial(1 - core), "c")
        return add(partial(core), received)

    met = swap_pairs(chip_sum(rows[:8]))
    total = add(chip_sum(rows[8:]), met)
    sums = jnp.sum(lax.all_to_all(total, PAIRS, 0, 0).astype(F32), axis=0)
    columns = [sums[size * k : size * k + size] for k in range(tiles)]
    return jnp.concatenate(columns, axis=1), sums[size * tiles, :size]


def on_device(
    tokens,
    norm_gain,
    in_x_weight,
    in_z_weight,
    conv_state,
    conv_weight,
    conv_bias,
    proj_weight,
    delta_weight,
    delta_bias,
    decay_log,
    ssm_state,
    skip_gain,
    out_weight,
    post_gain,
    gate_weight,
    up_weight,
    down_weight,
):
    core = lax.axis_index("c")
    inner_dev = in_x_weight.shape[1]
    own_rows = conv_state.shape[1]
    token_rows, token_cols = tokens.shape

    sums, first = reduce_rows(
        tokens, norm_gain, jnp.concatenate([in_x_weight, in_z_weight], axis=1)
    )
    scale = lax.rsqrt(first / WIDTH + epsilon)[:, None]
    inner_x = (sums[:, :inner_dev] * scale).astype(BF16)
    gate_z = (sums[:, inner_dev:] * scale).astype(BF16)
    window = jnp.concatenate([conv_state, inner_x[None]], axis=0)
    conv_pre = jnp.sum(window.astype(F32) * conv_weight[:, None, :], axis=0) + conv_bias[None, :]
    signal = jax.nn.silu(conv_pre).astype(BF16)
    projected = jnp.sum(
        spread(dot(signal, proj_weight).astype(BF16), TENSOR, 16).astype(F32), axis=0
    )
    delta_low = projected[:, :RANK]
    input_map = projected[:, RANK : RANK + STATE]
    output_map = projected[:, RANK + STATE :]
    delta_scale = lax.rsqrt(jnp.mean(delta_low * delta_low, axis=1, keepdims=True) + epsilon)
    delta_norm = (delta_low * delta_scale).astype(BF16)
    delta = jax.nn.softplus(dot(delta_norm, delta_weight) + delta_bias[None, :])
    signal_wide = signal.astype(F32)
    decay = jnp.exp(delta[:, None, :] * (-jnp.exp(decay_log))[None, :, :])
    new_state = decay * ssm_state + (delta * signal_wide)[:, None, :] * input_map[:, :, None]
    readout = jnp.sum(new_state * output_map[:, :, None], axis=1) + skip_gain[None, :] * signal_wide
    gated = (readout * jax.nn.silu(gate_z.astype(F32))).astype(BF16)

    dense = lax.optimization_barrier(gated).reshape(16, own_rows * inner_dev // 16)
    same = spread(dense, RING, 16).reshape(16, own_rows, inner_dev)
    same = lax.optimization_barrier(same)
    other = swap(same, "c")
    rows = jnp.concatenate(
        [jnp.where(core == 0, same, other), jnp.where(core == 0, other, same)], axis=1
    )
    out_terms = dot(rows.reshape(16 * token_rows, inner_dev), out_weight).astype(BF16)
    out_own = jnp.sum(
        lax.all_to_all(out_terms.reshape(16, token_rows, token_cols), TENSOR, 0, 0).astype(F32),
        axis=0,
    )
    residual = (tokens.astype(F32) + out_own).astype(BF16)

    sums, second = reduce_wide_rows(residual, post_gain, gate_weight, up_weight)
    scale = lax.rsqrt(second / WIDTH + epsilon)[:, None]
    hidden = gate_weight.shape[1] // 2
    both = sums * scale
    active = (jax.nn.silu(both[:, :hidden]) * both[:, hidden:]).astype(BF16)
    near = spread(active, PAIRS, 8)
    next_to = swap_pairs(near)
    own_part, other_part = half_rows(down_weight, core), half_rows(down_weight, 1 - core)

    def down(same, other):
        flat = (8 * token_rows, hidden)
        return dot(same.reshape(flat), own_part) + dot(other.reshape(flat), other_part)

    near_terms = down(near, swap(near, "c"))
    next_terms = down(next_to, swap(next_to, "c"))
    down_terms = jnp.concatenate([near_terms, next_terms], axis=0).astype(BF16)
    down_own = jnp.sum(
        exchange(down_terms.reshape(16, token_rows, token_cols), 0).astype(F32), axis=0
    )
    mixed = (residual.astype(F32) + down_own).astype(BF16)
    return (mixed, window[1:], new_state)


def solution(mesh):
    fine = Mesh(
        np.asarray(mesh.devices).reshape(4, 2, 2, 2, 4, 2, 2),
        ("zh", "zm", "zp", "c", "y", "xm", "xp"),
    )
    batch, tensor = ("zh", "zm", "zp", "c"), TENSOR
    return jax.shard_map(
        on_device,
        mesh=fine,
        in_specs=(
            P(tensor, batch),
            P(batch),
            P(batch, tensor),
            P(batch, tensor),
            P(None, batch, tensor),
            P(None, tensor),
            P(tensor),
            P(tensor, None),
            P(None, tensor),
            P(tensor),
            P(None, tensor),
            P(batch, None, tensor),
            P(tensor),
            P(tensor, batch),
            P(batch),
            P(batch, tensor),
            P(batch, tensor),
            P(tensor, batch),
        ),
        out_specs=(P(tensor, batch), P(None, batch, tensor), P(batch, None, tensor)),
        check_vma=False,
    )
```

```python
import jax
import jax.numpy as jnp
import numpy as np
from jax import lax
from jax.sharding import Mesh, PartitionSpec as P

WIDTH = 8192
RANK = 512
STATE = 16
TILE = 256

epsilon = 1e-06

F32 = jnp.float32
BF16 = jnp.bfloat16
TENSOR = ("y", "xm", "xp")
RING = ("zh", "zm", "zp")
PAIRS = ("zh", "zm")


def spread(block, axes, count):
    return lax.all_to_all(jnp.broadcast_to(block[None], (count,) + block.shape), axes, 0, 0)


def planes(first):
    groups = []
    for plane in range(32):
        parity = (plane // 2) % 2 ^ first
        tensor = list(range(parity, 16, 2)) + list(range(1 - parity, 16, 2))
        groups.append([16 * plane + place for place in tensor])
    return groups


def exchange(blocks, first):
    return lax.all_to_all(blocks, RING + ("c",) + TENSOR, 0, 0, axis_index_groups=planes(first))


def swap(block, axis):
    return lax.ppermute(block, axis, [(0, 1), (1, 0)])


def swap_pairs(block):
    moves = []
    for z in range(16):
        step = 1 if z % 2 == 0 else -1
        moves.append((2 * z, 2 * (z + step)))
        moves.append((2 * z + 1, 2 * ((z - step) % 16) + 1))
    return lax.ppermute(block, RING + ("c",), moves)


def dot(left, right):
    return jnp.dot(left, right, preferred_element_type=F32)


def add(left, right):
    return (left.astype(F32) + right.astype(F32)).astype(BF16)


def half_columns(weight, which):
    half = weight.shape[1] // 2
    return lax.dynamic_slice_in_dim(weight, which * half, half, 1)


def half_rows(block, which):
    half = block.shape[0] // 2
    return lax.dynamic_slice_in_dim(block, which * half, half, 0)


def spread_rows(block):
    return exchange(jnp.broadcast_to(block[None], (16,) + block.shape), 1)


def reduce_rows(block, gain, weight):
    first_core = lax.axis_index("c") == 0
    rows = spread_rows(block)
    size = rows.shape[1] // 2
    columns = weight.shape[1]
    padded = size + 4
    spare = lax.broadcasted_iota(jnp.int32, (1, padded, columns), 1) == size
    low, high = rows[:, :size], rows[:, size:]

    def partial(part):
        wide = jnp.pad(part, ((0, 0), (0, 4), (0, 0))).astype(F32)
        scaled = (wide * gain[None, None, :]).astype(BF16).reshape(16 * padded, -1)
        squares = jnp.sum(wide * wide, axis=2).astype(BF16)[:, None, :]
        marks = jnp.pad(squares, ((0, 0), (0, 0), (0, columns - padded)))
        return jnp.where(spare, marks, dot(scaled, weight).astype(BF16).reshape(16, padded, columns))

    received = swap(partial(jnp.where(first_core, high, low)), "c")
    both = add(partial(jnp.where(first_core, low, high)), received)
    total = add(both[8:], swap_pairs(both[:8]))
    sums = jnp.sum(lax.all_to_all(total, PAIRS, 0, 0).astype(F32), axis=0)
    return sums[:size], sums[size, :size]


def reduce_wide_rows(block, gain, left_weight, right_weight):
    core = lax.axis_index("c")
    size, depth = block.shape
    rows = spread_rows(block)
    wide = rows.astype(F32)
    scaled = (wide * gain[None, None, :]).astype(BF16).reshape(16 * size, depth)
    squares = jnp.sum(wide * wide, axis=2).astype(BF16)[:, None, :]
    marks = jnp.pad(squares, ((0, 0), (0, 7), (0, TILE - size)))
    tiles = left_weight.shape[1] // TILE

    def partial(which):
        weight = jnp.concatenate(
            [half_columns(left_weight, which), half_columns(right_weight, which)], axis=1
        )
        terms = dot(scaled, weight).astype(BF16).reshape(16, size, tiles * TILE)
        return jnp.concatenate(
            [terms[:, :, TILE * k : TILE * k + TILE] for k in range(tiles)] + [marks], axis=1
        )

    received = swap(partial(1 - core), "c")
    both = add(partial(core), received)
    total = add(both[8:], swap_pairs(both[:8]))
    sums = jnp.sum(lax.all_to_all(total, PAIRS, 0, 0).astype(F32), axis=0)
    columns = [sums[size * k : size * k + size] for k in range(tiles)]
    return jnp.concatenate(columns, axis=1), sums[size * tiles, :size]


def on_device(
    tokens,
    norm_gain,
    in_x_weight,
    in_z_weight,
    conv_state,
    conv_weight,
    conv_bias,
    proj_weight,
    delta_weight,
    delta_bias,
    decay_log,
    ssm_state,
    skip_gain,
    out_weight,
    post_gain,
    gate_weight,
    up_weight,
    down_weight,
):
    core = lax.axis_index("c")
    inner_dev = in_x_weight.shape[1]
    own_rows = conv_state.shape[1]
    token_rows, token_cols = tokens.shape

    sums, first = reduce_rows(
        tokens, norm_gain, jnp.concatenate([in_x_weight, in_z_weight], axis=1)
    )
    scale = lax.rsqrt(first / WIDTH + epsilon)[:, None]
    inner_x = (sums[:, :inner_dev] * scale).astype(BF16)
    gate_z = (sums[:, inner_dev:] * scale).astype(BF16)
    window = jnp.concatenate([conv_state, inner_x[None]], axis=0)
    conv_pre = jnp.sum(window.astype(F32) * conv_weight[:, None, :], axis=0) + conv_bias[None, :]
    signal = jax.nn.silu(conv_pre).astype(BF16)
    terms = dot(signal, proj_weight).astype(BF16)
    maps = jnp.pad(terms[:, RANK:].reshape(4, -1), ((0, 0), (0, RANK - 8 * own_rows)))
    packed = jnp.concatenate([terms[:, :RANK], maps], axis=0)
    projected = jnp.sum(spread(packed, TENSOR, 16).astype(F32), axis=0)
    delta_low = projected[:own_rows]
    maps = projected[own_rows:, : 8 * own_rows].reshape(own_rows, 2 * STATE)
    input_map, output_map = maps[:, :STATE], maps[:, STATE:]
    delta_scale = lax.rsqrt(jnp.mean(delta_low * delta_low, axis=1, keepdims=True) + epsilon)
    delta_norm = (delta_low * delta_scale).astype(BF16)
    delta = jax.nn.softplus(dot(delta_norm, delta_weight) + delta_bias[None, :])
    signal_wide = signal.astype(F32)
    decay = jnp.exp(delta[:, None, :] * (-jnp.exp(decay_log))[None, :, :])
    new_state = decay * ssm_state + (delta * signal_wide)[:, None, :] * input_map[:, :, None]
    readout = jnp.sum(new_state * output_map[:, :, None], axis=1) + skip_gain[None, :] * signal_wide
    gated = (readout * jax.nn.silu(gate_z.astype(F32))).astype(BF16)

    dense = lax.optimization_barrier(gated).reshape(16, own_rows * inner_dev // 16)
    same = spread(dense, RING, 16).reshape(16, own_rows, inner_dev)
    same = lax.optimization_barrier(same)
    other = swap(same, "c")
    rows = jnp.concatenate(
        [jnp.where(core == 0, same, other), jnp.where(core == 0, other, same)], axis=1
    )
    out_terms = dot(rows.reshape(16 * token_rows, inner_dev), out_weight).astype(BF16)
    out_own = jnp.sum(
        lax.all_to_all(out_terms.reshape(16, token_rows, token_cols), TENSOR, 0, 0).astype(F32),
        axis=0,
    )
    residual = (tokens.astype(F32) + out_own).astype(BF16)

    sums, second = reduce_wide_rows(residual, post_gain, gate_weight, up_weight)
    scale = lax.rsqrt(second / WIDTH + epsilon)[:, None]
    hidden = gate_weight.shape[1] // 2
    both = sums * scale
    active = (jax.nn.silu(both[:, :hidden]) * both[:, hidden:]).astype(BF16)
    near = spread(active, PAIRS, 8)
    next_to = swap_pairs(near)
    own_part, other_part = half_rows(down_weight, core), half_rows(down_weight, 1 - core)

    def down(same, other):
        flat = (8 * token_rows, hidden)
        return dot(same.reshape(flat), own_part) + dot(other.reshape(flat), other_part)

    near_terms = down(near, swap(near, "c"))
    next_terms = down(next_to, swap(next_to, "c"))
    down_terms = jnp.concatenate([near_terms, next_terms], axis=0).astype(BF16)
    down_own = jnp.sum(
        exchange(down_terms.reshape(16, token_rows, token_cols), 0).astype(F32), axis=0
    )
    mixed = (residual.astype(F32) + down_own).astype(BF16)
    return (mixed, window[1:], new_state)


def solution(mesh):
    fine = Mesh(
        np.asarray(mesh.devices).reshape(4, 2, 2, 2, 4, 2, 2),
        ("zh", "zm", "zp", "c", "y", "xm", "xp"),
    )
    batch, tensor = ("zh", "zm", "zp", "c"), TENSOR
    return jax.shard_map(
        on_device,
        mesh=fine,
        in_specs=(
            P(tensor, batch),
            P(batch),
            P(batch, tensor),
            P(batch, tensor),
            P(None, batch, tensor),
            P(None, tensor),
            P(tensor),
            P(tensor, None),
            P(None, tensor),
            P(tensor),
            P(None, tensor),
            P(batch, None, tensor),
            P(tensor),
            P(tensor, batch),
            P(batch),
            P(batch, tensor),
            P(batch, tensor),
            P(tensor, batch),
        ),
        out_specs=(P(tensor, batch), P(None, batch, tensor), P(batch, None, tensor)),
        check_vma=False,
    )
```

```python
import jax
import jax.numpy as jnp
import numpy as np
from jax import lax
from jax.sharding import Mesh, PartitionSpec as P

WIDTH = 8192
RANK = 512
STATE = 16
TILE = 256

epsilon = 1e-06

F32 = jnp.float32
BF16 = jnp.bfloat16
TENSOR = ("y", "xm", "xp")
RING = ("zh", "zm", "zp")
PAIRS = ("zh", "zm")


def spread(block, axes, count):
    return lax.all_to_all(jnp.broadcast_to(block[None], (count,) + block.shape), axes, 0, 0)


def planes(first):
    groups = []
    for plane in range(32):
        parity = (plane // 2) % 2 ^ first
        tensor = list(range(parity, 16, 2)) + list(range(1 - parity, 16, 2))
        groups.append([16 * plane + place for place in tensor])
    return groups


def exchange(blocks, first):
    return lax.all_to_all(blocks, RING + ("c",) + TENSOR, 0, 0, axis_index_groups=planes(first))


def swap(block, axis):
    return lax.ppermute(block, axis, [(0, 1), (1, 0)])


def swap_pairs(block):
    moves = []
    for z in range(16):
        step = 1 if z % 2 == 0 else -1
        moves.append((2 * z, 2 * (z + step)))
        moves.append((2 * z + 1, 2 * ((z - step) % 16) + 1))
    return lax.ppermute(block, RING + ("c",), moves)


def dot(left, right):
    return jnp.dot(left, right, preferred_element_type=F32)


def add(left, right):
    return (left.astype(F32) + right.astype(F32)).astype(BF16)


def half_columns(weight, which):
    half = weight.shape[1] // 2
    return lax.dynamic_slice_in_dim(weight, which * half, half, 1)


def half_rows(block, which):
    half = block.shape[0] // 2
    return lax.dynamic_slice_in_dim(block, which * half, half, 0)


def spread_rows(block):
    return exchange(jnp.broadcast_to(block[None], (16,) + block.shape), 1)


def reduce_rows(block, gain, weight):
    first_core = lax.axis_index("c") == 0
    rows = spread_rows(block)
    size = rows.shape[1] // 2
    columns = weight.shape[1]
    padded = size + 4
    spare = lax.broadcasted_iota(jnp.int32, (1, padded, columns), 1) == size
    low, high = rows[:, :size], rows[:, size:]

    def partial(part):
        wide = jnp.pad(part, ((0, 0), (0, 4), (0, 0))).astype(F32)
        scaled = (wide * gain[None, None, :]).astype(BF16).reshape(16 * padded, -1)
        squares = jnp.sum(wide * wide, axis=2).astype(BF16)[:, None, :]
        marks = jnp.pad(squares, ((0, 0), (0, 0), (0, columns - padded)))
        return jnp.where(spare, marks, dot(scaled, weight).astype(BF16).reshape(16, padded, columns))

    received = swap(partial(jnp.where(first_core, high, low)), "c")
    both = add(partial(jnp.where(first_core, low, high)), received)
    total = add(both[8:], swap_pairs(both[:8]))
    sums = jnp.sum(lax.all_to_all(total, PAIRS, 0, 0).astype(F32), axis=0)
    return sums[:size], sums[size, :size]


def reduce_wide_rows(block, gain, left_weight, right_weight):
    core = lax.axis_index("c")
    size, depth = block.shape
    rows = spread_rows(block)
    wide = rows.astype(F32)
    scaled = (wide * gain[None, None, :]).astype(BF16).reshape(16 * size, depth)
    squares = jnp.sum(wide * wide, axis=2).astype(BF16)[:, None, :]
    marks = jnp.pad(squares, ((0, 0), (0, 7), (0, TILE - size)))
    tiles = left_weight.shape[1] // TILE

    def partial(which):
        weight = jnp.concatenate(
            [half_columns(left_weight, which), half_columns(right_weight, which)], axis=1
        )
        terms = dot(scaled, weight).astype(BF16).reshape(16, size, tiles * TILE)
        return jnp.concatenate(
            [terms[:, :, TILE * k : TILE * k + TILE] for k in range(tiles)] + [marks], axis=1
        )

    received = swap(partial(1 - core), "c")
    both = add(partial(core), received)
    total = add(both[8:], swap_pairs(both[:8]))
    sums = jnp.sum(lax.all_to_all(total, PAIRS, 0, 0).astype(F32), axis=0)
    columns = [sums[size * k : size * k + size] for k in range(tiles)]
    return jnp.concatenate(columns, axis=1), sums[size * tiles, :size]


def on_device(
    tokens,
    norm_gain,
    in_x_weight,
    in_z_weight,
    conv_state,
    conv_weight,
    conv_bias,
    proj_weight,
    delta_weight,
    delta_bias,
    decay_log,
    ssm_state,
    skip_gain,
    out_weight,
    post_gain,
    gate_weight,
    up_weight,
    down_weight,
):
    core = lax.axis_index("c")
    inner_dev = in_x_weight.shape[1]
    own_rows = conv_state.shape[1]
    token_rows, token_cols = tokens.shape

    sums, first = reduce_rows(
        tokens, norm_gain, jnp.concatenate([in_x_weight, in_z_weight], axis=1)
    )
    scale = lax.rsqrt(first / WIDTH + epsilon)[:, None]
    inner_x = (sums[:, :inner_dev] * scale).astype(BF16)
    gate_z = (sums[:, inner_dev:] * scale).astype(BF16)
    window = jnp.concatenate([conv_state, inner_x[None]], axis=0)
    conv_pre = jnp.sum(window.astype(F32) * conv_weight[:, None, :], axis=0) + conv_bias[None, :]
    signal = jax.nn.silu(conv_pre).astype(BF16)
    terms = dot(signal, proj_weight).astype(BF16)
    maps = jnp.pad(terms[:, RANK:].reshape(4, -1), ((0, 0), (0, RANK - 8 * own_rows)))
    packed = jnp.concatenate([terms[:, :RANK], maps], axis=0)
    projected = jnp.sum(spread(packed, TENSOR, 16).astype(F32), axis=0)
    delta_low = projected[:own_rows]
    maps = projected[own_rows:, : 8 * own_rows].reshape(own_rows, 2 * STATE)
    input_map, output_map = maps[:, :STATE], maps[:, STATE:]
    delta_scale = lax.rsqrt(jnp.mean(delta_low * delta_low, axis=1, keepdims=True) + epsilon)
    delta_norm = (delta_low * delta_scale).astype(BF16)
    delta = jax.nn.softplus(dot(delta_norm, delta_weight) + delta_bias[None, :])
    signal_wide = signal.astype(F32)
    decay = jnp.exp(delta[:, None, :] * (-jnp.exp(decay_log))[None, :, :])
    new_state = decay * ssm_state + (delta * signal_wide)[:, None, :] * input_map[:, :, None]
    readout = jnp.sum(new_state * output_map[:, :, None], axis=1) + skip_gain[None, :] * signal_wide
    gated = (readout * jax.nn.silu(gate_z.astype(F32))).astype(BF16)

    dense = lax.optimization_barrier(gated).reshape(16, own_rows * inner_dev // 16)
    same = spread(dense, RING, 16).reshape(16, own_rows, inner_dev)
    same = lax.optimization_barrier(same)
    other = swap(same, "c")
    rows = jnp.concatenate([same, other], axis=1)
    out_terms = dot(rows.reshape(16 * token_rows, inner_dev), out_weight).astype(BF16)
    out_sum = jnp.sum(
        lax.all_to_all(out_terms.reshape(16, token_rows, token_cols), TENSOR, 0, 0).astype(F32),
        axis=0,
    )
    turned = jnp.concatenate([out_sum[own_rows:], out_sum[:own_rows]], axis=0)
    out_own = jnp.where(core == 0, out_sum, turned)
    residual = (tokens.astype(F32) + out_own).astype(BF16)

    sums, second = reduce_wide_rows(residual, post_gain, gate_weight, up_weight)
    scale = lax.rsqrt(second / WIDTH + epsilon)[:, None]
    hidden = gate_weight.shape[1] // 2
    both = sums * scale
    active = (jax.nn.silu(both[:, :hidden]) * both[:, hidden:]).astype(BF16)
    near = spread(active, PAIRS, 8)
    next_to = swap_pairs(near)
    own_part, other_part = half_rows(down_weight, core), half_rows(down_weight, 1 - core)

    def down(same, other):
        flat = (8 * token_rows, hidden)
        return dot(same.reshape(flat), own_part) + dot(other.reshape(flat), other_part)

    near_terms = down(near, swap(near, "c"))
    next_terms = down(next_to, swap(next_to, "c"))
    down_terms = jnp.concatenate([near_terms, next_terms], axis=0).astype(BF16)
    down_own = jnp.sum(
        exchange(down_terms.reshape(16, token_rows, token_cols), 0).astype(F32), axis=0
    )
    mixed = (residual.astype(F32) + down_own).astype(BF16)
    return (mixed, window[1:], new_state)


def solution(mesh):
    fine = Mesh(
        np.asarray(mesh.devices).reshape(4, 2, 2, 2, 4, 2, 2),
        ("zh", "zm", "zp", "c", "y", "xm", "xp"),
    )
    batch, tensor = ("zh", "zm", "zp", "c"), TENSOR
    return jax.shard_map(
        on_device,
        mesh=fine,
        in_specs=(
            P(tensor, batch),
            P(batch),
            P(batch, tensor),
            P(batch, tensor),
            P(None, batch, tensor),
            P(None, tensor),
            P(tensor),
            P(tensor, None),
            P(None, tensor),
            P(tensor),
            P(None, tensor),
            P(batch, None, tensor),
            P(tensor),
            P(tensor, batch),
            P(batch),
            P(batch, tensor),
            P(batch, tensor),
            P(tensor, batch),
        ),
        out_specs=(P(tensor, batch), P(None, batch, tensor), P(batch, None, tensor)),
        check_vma=False,
    )
```
